128 devices in a mesh: blk: 4 (over z), grp: 32 (over x, y, core).
Axes of the slice: x: 4, y: 4, z: 4, core: 2. Of those that a mesh axis runs over, the one named last changes fastest.
Arguments:
- loads: float32 [524288, 256], P(('blk', 'grp')), may hold values from -45 to 45
- pore_diag: float32 [524288], P(('blk', 'grp')), may hold values from 2 to 8
- near_blocks: float32 [12288, 128, 128], P(('blk', 'grp')), may hold values from -0.125 to 0.125
- near_cols: int32 [12288], P(('blk', 'grp')), may hold values from 0 to 39
- short_blocks: float32 [512, 2, 128, 128], P(('blk', 'grp')), may hold values from -0.125 to 0.125
- short_rows: int32 [512, 2], P(('blk', 'grp')), may hold values from 0 to 31
- short_cols: int32 [512, 2], P(('blk', 'grp')), may hold values from 0 to 31
Outputs:
- solution: float32 [524288, 256], P(('blk', 'grp'))
- residual: float32 [524288, 256], P(('blk', 'grp'))
The draws below stay inside these ranges and needn't reach their ends.
All inputs are finite; a program needn't handle non-finite values.
Results may differ from the reference program's by a relative error of at most 0.0003.
Values sent between devices are 32-bit elements; how exact they have to be, the bound alone decides.
A program may use at most 192 MiB of HBM per device.

```python
import math
import jax
import jax.numpy as jnp
from jax import lax

BLOCK = 128
CASES = 256
BR_DEV = 32
NEAR_PER = 3
HB = 4
SHORT = 2
NPORES = 524288
N_BLK = 4
N_GRP = 32


def draw_loads(key, part):
    key = jax.random.fold_in(key, 17)
    key_rows = jax.random.fold_in(key, 0)
    key_cols = jax.random.fold_in(key, 1)
    key_noise = jax.random.fold_in(key, 2)
    key_left = jax.random.fold_in(key, 4)
    key_right = jax.random.fold_in(key, 5)
    key_strength = jax.random.fold_in(key, 6)
    shared_count = max(2, CASES // 8)
    row_scale = jnp.exp(jax.random.uniform(key_rows, (NPORES, 1), jnp.float32, math.log(0.3), math.log(3.0)))
    col_scale = jnp.exp(jax.random.uniform(key_cols, (1, CASES), jnp.float32, math.log(0.3), math.log(3.0)))
    shared_left = jnp.clip(jax.random.normal(key_left, (NPORES, shared_count), jnp.float32), -3.0, 3.0)
    shared_right = jnp.clip(jax.random.normal(key_right, (shared_count, CASES), jnp.float32), -3.0, 3.0)
    noise_part = jnp.clip(jax.random.normal(key_noise, (NPORES, CASES), jnp.float32), -5.0, 5.0)
    strength = jnp.exp(jax.random.uniform(key_strength, (shared_count,), jnp.float32, math.log(0.08), math.log(0.5)))
    shared_part = jnp.zeros((NPORES, CASES), jnp.float32)
    for component in range(shared_count):
        shared_part = shared_part + strength[component] * shared_left[:, component:component + 1] * shared_right[component:component + 1, :]
    return jnp.clip((noise_part + shared_part) * row_scale * col_scale, -45.0, 45.0).astype(jnp.float32)


def set_ends(values, key, smallest, largest):
    spot = [jax.random.randint(jax.random.fold_in(key, axis), (), 0, length) for axis, length in enumerate(values.shape)]
    main_axis = values.shape.index(max(values.shape))
    next_to = spot[:main_axis] + [(spot[main_axis] + 1) % values.shape[main_axis]] + spot[main_axis + 1:]
    return values.at[tuple(spot)].set(smallest).at[tuple(next_to)].set(largest)


def block_scale(own_key, extent, cuts, least, high):
    factor_of, own = 1.0, jax.random.fold_in(own_key, 6)
    for axis_at, parts in cuts:
        draws = jnp.exp(jax.random.uniform(jax.random.fold_in(own, axis_at), (parts,), jnp.float32, least / len(cuts), high / len(cuts)))
        factor_of = factor_of * jnp.repeat(draws, extent[axis_at] // parts).reshape([-1 if axis == axis_at else 1 for axis in range(len(extent))])
    return factor_of


def normal_values(own_key, shape, deviation, limit, cuts=(), held_as=jnp.bfloat16):
    values = deviation * jax.random.normal(own_key, shape, jnp.float32)
    if cuts:
        values = values * block_scale(own_key, shape, cuts, -0.22, 0.18)
    return jnp.clip(values, -limit, limit).astype(held_as)


def setup_inputs(seed: int = 0) -> dict:
    arg_keys = jax.random.split(jax.random.key(seed), 8)
    loads = draw_loads(jax.random.fold_in(arg_keys[7], 71), 0)
    pore_diag = jnp.clip(jnp.exp(math.log(8.0) - 1.3862944 * jax.random.uniform(arg_keys[1], (NPORES,), jnp.float32) ** block_scale(arg_keys[1], (NPORES,), ((0, 128),), -0.2, 0.2)), 2.0, 8.0)
    near_blocks = normal_values(arg_keys[2], (N_BLK * N_GRP * BR_DEV * NEAR_PER, BLOCK, BLOCK), (16 * BLOCK) ** -0.5, 0.125, ((0, 128),), jnp.float32)
    near_cols = set_ends(jax.random.randint(arg_keys[3], (N_BLK * N_GRP * BR_DEV * NEAR_PER,), 0, BR_DEV + 2 * HB), jax.random.fold_in(arg_keys[3], 1), 0, (BR_DEV + 2 * HB) - 1).astype(jnp.int32)
    short_blocks = normal_values(arg_keys[4], (N_BLK * N_GRP * N_BLK, SHORT, BLOCK, BLOCK), (16 * BLOCK) ** -0.5, 0.125, ((0, 128),), jnp.float32)
    short_rows = set_ends(jax.random.randint(arg_keys[5], (N_BLK * N_GRP * N_BLK, SHORT), 0, BR_DEV), jax.random.fold_in(arg_keys[5], 1), 0, BR_DEV - 1).astype(jnp.int32)
    short_cols = set_ends(jax.random.randint(arg_keys[6], (N_BLK * N_GRP * N_BLK, SHORT), 0, BR_DEV), jax.random.fold_in(arg_keys[6], 1), 0, BR_DEV - 1).astype(jnp.int32)
    return {"loads": loads, "pore_diag": pore_diag, "near_blocks": near_blocks, "near_cols": near_cols, "short_blocks": short_blocks, "short_rows": short_rows, "short_cols": short_cols}


HIGH = lax.Precision.HIGHEST

def chol_solve(matrix, rhs):
    factor = jnp.linalg.cholesky(matrix)
    middle = lax.linalg.triangular_solve(factor, rhs, left_side=True, lower=True)
    return lax.linalg.triangular_solve(factor, middle, left_side=True, lower=True, transpose_a=True)

def inner(left, right):
    return jnp.einsum('nc,nd->cd', left, right, precision=HIGH)

def near_sector(sector, blocks, cols):
    total = sector.shape[0]
    stored = jnp.arange(total * NEAR_PER, dtype=jnp.int32)
    row_pos = stored // NEAR_PER
    slab = row_pos // BR_DEV
    col_pos = (slab * BR_DEV + cols.astype(jnp.int32) - HB) % total
    forward = jnp.einsum('kab,kbn->kan', blocks, sector[col_pos], precision=HIGH)
    backward = jnp.einsum('kba,kbn->kan', blocks, sector[row_pos], precision=HIGH)
    return jnp.zeros_like(sector).at[row_pos].add(forward).at[col_pos].add(backward)

def apply_operator(field, pore_diag, near_blocks, near_cols, short_blocks, short_rows, short_cols):
    sectors = field.reshape(N_BLK, N_GRP * BR_DEV, BLOCK, CASES)
    near_all = lax.map(lambda xs: near_sector(xs[0], xs[1], xs[2]), (sectors, near_blocks.reshape(N_BLK, N_GRP * BR_DEV * NEAR_PER, BLOCK, BLOCK), near_cols.reshape(N_BLK, N_GRP * BR_DEV * NEAR_PER)))
    grid = field.reshape(N_BLK, N_GRP, BR_DEV, BLOCK, CASES)
    mats = short_blocks.reshape(N_BLK, N_GRP, N_BLK, SHORT, BLOCK, BLOCK)
    rows_idx = short_rows.reshape(N_BLK, N_GRP, N_BLK, SHORT).astype(jnp.int32)
    cols_idx = short_cols.reshape(N_BLK, N_GRP, N_BLK, SHORT).astype(jnp.int32)
    shape = rows_idx.shape
    sector_idx = jnp.broadcast_to(jnp.arange(N_BLK, dtype=jnp.int32)[:, None, None, None], shape)
    slab_idx = jnp.broadcast_to(jnp.arange(N_GRP, dtype=jnp.int32)[None, :, None, None], shape)
    target_idx = jnp.broadcast_to(jnp.arange(N_BLK, dtype=jnp.int32)[None, None, :, None], shape)
    partner = grid[target_idx, slab_idx, cols_idx]
    own_rows = grid[sector_idx, slab_idx, rows_idx]
    reach = jnp.einsum('bgcsij,bgcsjn->bgcsin', mats, partner, precision=HIGH)
    sent = jnp.einsum('bgcsji,bgcsjn->bgcsin', mats, own_rows, precision=HIGH)
    short_all = jnp.zeros_like(grid).at[sector_idx, slab_idx, rows_idx].add(reach)
    short_all = short_all.at[target_idx, slab_idx, cols_idx].add(sent)
    return pore_diag[:, None] * field + near_all.reshape(field.shape) + short_all.reshape(field.shape)

def reference(loads, pore_diag, near_blocks, near_cols, short_blocks, short_rows, short_cols):

    def operate(field):
        return apply_operator(field, pore_diag, near_blocks, near_cols, short_blocks, short_rows, short_cols)
    resid_zero = loads
    search_zero = loads
    rr_zero = inner(resid_zero, resid_zero)
    image_one = operate(search_zero)
    gram_one = inner(search_zero, image_one)
    pq_one = 0.5 * (gram_one + gram_one.T)
    alpha_one = chol_solve(pq_one, rr_zero)
    sol_one = jnp.dot(search_zero, alpha_one, precision=HIGH)
    resid_one = resid_zero - jnp.dot(image_one, alpha_one, precision=HIGH)
    rr_one = inner(resid_one, resid_one)
    beta_one = chol_solve(rr_zero, rr_one)
    search_one = resid_one + jnp.dot(search_zero, beta_one, precision=HIGH)
    image_two = operate(search_one)
    gram_two = inner(search_one, image_two)
    pq_two = 0.5 * (gram_two + gram_two.T)
    alpha_two = chol_solve(pq_two, rr_one)
    solution = sol_one + jnp.dot(search_one, alpha_two, precision=HIGH)
    residual = resid_one - jnp.dot(image_two, alpha_two, precision=HIGH)
    return (solution, residual)
```

```python
import functools

import jax
import jax.numpy as jnp
from jax import lax
from jax.experimental import pallas as pl
from jax.experimental.pallas import tpu as pltpu
from jax.sharding import PartitionSpec as P

NEAR_PER = 3
HB = 4
SHORT = 2
N_BLK = 4
MESH = pl.DeviceIdType.MESH
HIGH = lax.Precision.HIGHEST
F32 = jnp.float32
BF16 = jnp.bfloat16
VMEM_LIMIT = 60 * 1024 * 1024

PERM, KEEP, LAST, SPERM, SKEEP, SLAST, PLAN = 0, 96, 192, 240, 248, 256, 320


def split(x):
    hi = x.astype(BF16)
    lo = (x - hi.astype(F32)).astype(BF16)
    return hi, lo


def dot(a, b):
    return jnp.dot(a, b, preferred_element_type=F32)


def dot_t(a, b):
    return lax.dot_general(a, b, (((0,), (0,)), ((), ())), preferred_element_type=F32)


def plan_kernel(cols_ref, rows_ref, scols_ref, plan_ref, tile_ref, count, start):
    def order(keys, n_keys, n_dest, perm_at, keep_at, last_at):
        def clear(q, c):
            count[q] = 0
            return c

        lax.fori_loop(0, n_dest, clear, 0)

        def tally(m, c):
            q = keys(m)
            count[q] = count[q] + 1
            return c

        lax.fori_loop(0, n_keys, tally, 0)

        def prefix(q, run):
            start[q] = run
            end = run + count[q]
            plan_ref[last_at + q] = jnp.where(count[q] > 0, end, 0)
            count[q] = run
            return end

        lax.fori_loop(0, n_dest, prefix, jnp.int32(0))

        def place(m, c):
            q = keys(m)
            p = start[q]
            start[q] = p + 1
            plan_ref[perm_at + p] = m
            plan_ref[keep_at + p] = jnp.where(p > count[q], 1, 0)
            return c

        lax.fori_loop(0, n_keys, place, 0)

    order(lambda m: cols_ref[m], 96, 40, PERM, KEEP, LAST)
    order(lambda m: rows_ref[m], 8, 32, SPERM, SKEEP, SLAST)
    row = lax.broadcasted_iota(jnp.int32, (8, 128), 0)
    lane = lax.broadcasted_iota(jnp.int32, (8, 128), 1)
    tile = jnp.zeros((8, 128), jnp.int32)
    for c in range(N_BLK):
        for s in range(SHORT):
            tile = jnp.where((row == c) & (lane == s), scols_ref[c * SHORT + s], tile)
    tile_ref[...] = tile


def make_plan(near_cols, short_rows, short_cols):
    smem = pl.BlockSpec(memory_space=pltpu.SMEM)
    return pl.pallas_call(
        plan_kernel,
        out_shape=(
            jax.ShapeDtypeStruct((PLAN,), jnp.int32),
            jax.ShapeDtypeStruct((8, 128), jnp.int32),
        ),
        in_specs=[smem, smem, smem],
        out_specs=(smem, pl.BlockSpec(memory_space=pltpu.VMEM)),
        scratch_shapes=[pltpu.SMEM((48,), jnp.int32), pltpu.SMEM((48,), jnp.int32)],
        name="plan",
    )(near_cols, short_rows.reshape(-1), short_cols.reshape(-1))


def apply_kernel(
    plan, scols, field, diag, near, short, tile,
    image, grams,
    fv, ext, wn, ws, seg, out, halo, rim_out, rim_in, trm_out, trm, fet_out, fet, rseg,
    idx_in, idx_sm, acc_h, acc_l, acc_y,
    load_sem, out_sem, idx_sem, halo_send, halo_recv, idx_send, idx_recv, trm_send, trm_recv,
    fet_send, fet_recv, rim_send, rim_recv,
):
    brows = field.shape[0]
    b = lax.axis_index("blk")
    g = lax.axis_index("grp")
    n_grp = lax.axis_size("grp")
    left = (b, lax.rem(g + n_grp - 1, n_grp))
    right = (b, lax.rem(g + 1, n_grp))
    peers = [None] + [(lax.rem(b + d, N_BLK), g) for d in range(1, N_BLK)]

    loads = [
        pltpu.make_async_copy(field, fv, load_sem.at[0]),
        pltpu.make_async_copy(short, ws, load_sem.at[1]),
        pltpu.make_async_copy(near, wn, load_sem.at[2]),
    ]
    for copy in loads:
        copy.start()

    barrier = pltpu.get_barrier_semaphore()
    for peer in [left, right] + peers[1:]:
        pl.semaphore_signal(barrier, inc=1, device_id=peer, device_id_type=MESH)
    pl.semaphore_wait(barrier, 5)

    def remote(src, dst, send, recv, peer):
        copy = pltpu.make_async_remote_copy(
            src_ref=src, dst_ref=dst, send_sem=send, recv_sem=recv,
            device_id=peer, device_id_type=MESH,
        )
        copy.start()
        return copy

    idx_copies = [
        remote(tile, idx_in.at[3 - d], idx_send.at[d - 1], idx_recv.at[3 - d], peers[d])
        for d in range(1, N_BLK)
    ]
    halo_copies = [
        remote(field.at[pl.ds(0, HB)], halo.at[pl.ds(HB, HB)], halo_send.at[0], halo_recv.at[0], left),
        remote(field.at[pl.ds(brows - HB, HB)], halo.at[pl.ds(0, HB)], halo_send.at[1], halo_recv.at[1], right),
    ]

    loads[0].wait()
    loads[1].wait()

    def split_own(r, c):
        hi, lo = split(fv[r])
        ext[HB + r, :128, :] = hi
        ext[HB + r, 128:, :] = lo
        return c

    lax.fori_loop(0, brows, split_own, 0)

    def three(w, e):
        hi, lo = split(w)
        return dot(jnp.concatenate([hi, hi, lo], axis=1), jnp.concatenate([e, e[:128]], axis=0))

    for d in range(N_BLK):
        c = lax.rem(b + d, N_BLK)
        for s in range(SHORT):
            n = c * SHORT + s
            e = ext[HB + plan_rows(scols, n)]
            term = three(ws[n].T, e)
            if d == 0:
                trm[s] = term
            else:
                trm_out[(d - 1) * SHORT + s] = term
    trm_copies = []
    for d in (1, 3, 2):
        trm_copies.append(
            remote(
                trm_out.at[pl.ds((d - 1) * SHORT, SHORT)], trm.at[pl.ds((4 - d) * SHORT, SHORT)],
                trm_send.at[d - 1], trm_recv.at[3 - d], peers[d],
            )
        )

    for copy in idx_copies:
        copy.wait()
    local = pltpu.make_async_copy(idx_in, idx_sm, idx_sem)
    local.start()
    local.wait()
    for d in range(N_BLK):
        for s in range(SHORT):
            if d == 0:
                fet[s] = fv[scols[8 + b * SHORT + s]]
            else:
                fet_out[(d - 1) * SHORT + s] = fv[idx_sm[d - 1, b, s]]
    fet_copies = []
    for d in (1, 3, 2):
        fet_copies.append(
            remote(
                fet_out.at[pl.ds((d - 1) * SHORT, SHORT)], fet.at[pl.ds((4 - d) * SHORT, SHORT)],
                fet_send.at[d - 1], fet_recv.at[3 - d], peers[d],
            )
        )

    loads[2].wait()
    seg[0] = jnp.zeros(seg.shape[1:], F32)

    def backward(i, carry):
        for u in range(2):
            k = i * 2 + u
            m = plan[PERM + k]
            keep = plan[KEEP + k].astype(F32)
            term = three(wn[m].T, ext[HB + lax.div(m, NEAR_PER)])
            seg[k + 1] = seg[k] * keep + term
        return carry

    lax.fori_loop(0, brows * NEAR_PER // 2, backward, 0)
    for q in range(HB):
        rim_out[q] = seg[plan[LAST + q]]
        rim_out[HB + q] = seg[plan[LAST + HB + brows + q]]
    rim_copies = [
        remote(rim_out.at[pl.ds(0, HB)], rim_in.at[pl.ds(HB, HB)], rim_send.at[0], rim_recv.at[0], left),
        remote(rim_out.at[pl.ds(HB, HB)], rim_in.at[pl.ds(0, HB)], rim_send.at[1], rim_recv.at[1], right),
    ]

    acc_h[...] = jnp.zeros(acc_h.shape, F32)
    acc_l[...] = jnp.zeros(acc_l.shape, F32)
    acc_y[...] = jnp.zeros(acc_y.shape, F32)
    per = 4

    def gram(i, c):
        hi = ext[pl.ds(HB + i * per, per), :128, :].reshape(per * 128, 256)
        lo = ext[pl.ds(HB + i * per, per), 128:, :].reshape(per * 128, 256)
        acc_h[...] += dot_t(hi, hi)
        acc_l[...] += dot_t(hi, lo)
        acc_h[...] += dot_t(lo, lo)
        return c

    lax.fori_loop(0, brows // per, gram, 0)

    for copy in halo_copies:
        copy.wait()

    def split_halo(q, c):
        hi, lo = split(halo[q])
        at = jnp.where(q < HB, q, q + brows)
        ext[at, :128, :] = hi
        ext[at, 128:, :] = lo
        return c

    lax.fori_loop(0, 2 * HB, split_halo, 0)

    def half_diag(r):
        d = jnp.broadcast_to(diag[pl.ds(r, 1), :], (128, 128)).T * 0.5
        return jnp.concatenate([d, d], axis=1) * fv[r]

    def forward(r, c):
        lhs, rhs = [], []
        for j in range(NEAR_PER):
            m = r * NEAR_PER + j
            hi, lo = split(wn[m])
            e = ext[scols[16 + m]]
            lhs += [hi, hi, lo]
            rhs += [e, e[:128]]
        out[r] = half_diag(r) + dot(jnp.concatenate(lhs, axis=1), jnp.concatenate(rhs, axis=0))
        return c

    lax.fori_loop(0, brows, forward, 0)

    for copy in fet_copies:
        copy.wait()
    rseg[0] = jnp.zeros(rseg.shape[1:], F32)
    for i in range(N_BLK * SHORT):
        n = plan[SPERM + i]
        slot = lax.rem(lax.div(n, SHORT) + N_BLK - b, N_BLK) * SHORT + lax.rem(n, SHORT)
        hi, lo = split(fet[slot])
        term = three(ws[n], jnp.concatenate([hi, lo], axis=0))
        rseg[i + 1] = rseg[i] * plan[SKEEP + i].astype(F32) + term

    def gram_y(i, c):
        parts = []
        for u in range(per):
            r = i * per + u
            f = out[r] + rseg[plan[SLAST + r]]
            out[r] = f
            parts.append(f)
        fh, fl = split(jnp.concatenate(parts, axis=0))
        hi = ext[pl.ds(HB + i * per, per), :128, :].reshape(per * 128, 256)
        lo = ext[pl.ds(HB + i * per, per), 128:, :].reshape(per * 128, 256)
        acc_y[...] += dot_t(hi, fh) + dot_t(hi, fl) + dot_t(lo, fh)
        return c

    lax.fori_loop(0, brows // per, gram_y, 0)
    low = acc_l[...]
    grams[0] = acc_h[...] + (low + low.T)
    y = acc_y[...]
    grams[1] = y + y.T

    for copy in trm_copies:
        copy.wait()
    dest = [scols[8 + b * SHORT + s] for s in range(SHORT)]
    for d in range(1, N_BLK):
        dest += [idx_sm[d - 1, b, s] for s in range(SHORT)]

    def finish(r, c):
        total = out[r] + half_diag(r) + seg[plan[LAST + HB + r]]
        for i in range(N_BLK * SHORT):
            total += trm[i] * jnp.where(dest[i] == r, 1.0, 0.0)
        out[r] = total
        return c

    lax.fori_loop(0, brows, finish, 0)
    for copy in rim_copies:
        copy.wait()
    for q in range(HB):
        out[q] = out[q] + rim_in[q]
        out[brows - HB + q] = out[brows - HB + q] + rim_in[HB + q]
    copy = pltpu.make_async_copy(out, image, out_sem)
    copy.start()
    copy.wait()


def plan_rows(scols, n):
    return scols[n]


def apply(plan, scols, field, diag, near, short, tile):
    brows = field.shape[0]
    smem = pl.BlockSpec(memory_space=pltpu.SMEM)
    vmem = pl.BlockSpec(memory_space=pltpu.VMEM)
    hbm = pl.BlockSpec(memory_space=pl.ANY)
    block = lambda n: pltpu.VMEM((n, 128, 256), F32)
    dma = pltpu.SemaphoreType.DMA
    return pl.pallas_call(
        apply_kernel,
        out_shape=(
            jax.ShapeDtypeStruct(field.shape, F32),
            jax.ShapeDtypeStruct((2, 256, 256), F32),
        ),
        in_specs=[smem, smem, hbm, vmem, hbm, hbm, vmem],
        out_specs=(hbm, vmem),
        scratch_shapes=[
            block(brows),
            pltpu.VMEM((brows + 2 * HB, 256, 256), BF16),
            pltpu.VMEM(near.shape, F32),
            pltpu.VMEM(short.shape, F32),
            block(brows * NEAR_PER + 1),
            block(brows),
            block(2 * HB), block(2 * HB), block(2 * HB),
            block(6), block(8), block(6), block(8), block(9),
            pltpu.VMEM((3, 8, 128), jnp.int32),
            pltpu.SMEM((3, 8, 128), jnp.int32),
            pltpu.VMEM((256, 256), F32), pltpu.VMEM((256, 256), F32), pltpu.VMEM((256, 256), F32),
            dma((3,)), dma, dma,
            dma((2,)), dma((2,)), dma((3,)), dma((3,)), dma((3,)), dma((3,)), dma((3,)), dma((3,)),
            dma((2,)), dma((2,)),
        ],
        compiler_params=pltpu.CompilerParams(
            collective_id=0, has_side_effects=True, vmem_limit_bytes=VMEM_LIMIT
        ),
        name="apply",
    )(plan, scols, field, diag, near, short, tile)


def reduce_kernel(x, res, buf_a, part, buf_b, mid, sa, ra, sb, rb, sc, rc, sd, rd):
    b = lax.axis_index("blk")
    g = lax.axis_index("grp")
    n_grp = lax.axis_size("grp")
    core = lax.rem(g, 2)
    plane = lax.div(g, 2)
    n_a, n_b = N_BLK * 2, n_grp // 2
    a = b * 2 + core
    rows_a = x.shape[0] // n_a
    rows_b = rows_a // n_b
    a_peers = []
    for i in range(1, n_a):
        t = lax.rem(a + i, n_a)
        a_peers.append((t, (lax.div(t, 2), plane * 2 + lax.rem(t, 2))))
    b_peers = []
    for i in range(1, n_b):
        t = lax.rem(plane + i, n_b)
        b_peers.append((t, (b, t * 2 + core)))

    barrier = pltpu.get_barrier_semaphore()
    for _, peer in a_peers + b_peers:
        pl.semaphore_signal(barrier, inc=1, device_id=peer, device_id_type=MESH)
    pl.semaphore_wait(barrier, len(a_peers) + len(b_peers))

    def remote(src, dst, send, recv, peer):
        copy = pltpu.make_async_remote_copy(
            src_ref=src, dst_ref=dst, send_sem=send, recv_sem=recv,
            device_id=peer, device_id_type=MESH,
        )
        copy.start()
        return copy

    def piece(ref, at, rows):
        return ref.at[pl.ds(pl.multiple_of(at * rows, rows), rows)]

    copies = []
    for i, (t, peer) in enumerate(a_peers):
        copies.append(remote(piece(x, t, rows_a), buf_a.at[n_a - 2 - i], sa.at[i], ra.at[n_a - 2 - i], peer))
    total = x[pl.ds(pl.multiple_of(a * rows_a, rows_a), rows_a)]
    for copy in copies:
        copy.wait()
    for i in range(n_a - 1):
        total += buf_a[i]
    part[...] = total

    copies = []
    for i, (t, peer) in enumerate(b_peers):
        copies.append(remote(piece(part, t, rows_b), buf_b.at[n_b - 2 - i], sb.at[i], rb.at[n_b - 2 - i], peer))
    total = part[pl.ds(pl.multiple_of(plane * rows_b, rows_b), rows_b)]
    for copy in copies:
        copy.wait()
    for i in range(n_b - 1):
        total += buf_b[i]
    mid[pl.ds(pl.multiple_of(plane * rows_b, rows_b), rows_b)] = total

    copies = []
    for i, (t, peer) in enumerate(b_peers):
        copies.append(remote(piece(mid, plane, rows_b), piece(mid, plane, rows_b), sc.at[i], rc.at[n_b - 2 - i], peer))
    for copy in copies:
        copy.wait()

    res[pl.ds(pl.multiple_of(a * rows_a, rows_a), rows_a)] = mid[...]
    copies = []
    for i, (t, peer) in enumerate(a_peers):
        copies.append(remote(mid, piece(res, a, rows_a), sd.at[i], rd.at[n_a - 2 - i], peer))
    for copy in copies:
        copy.wait()


def reduce_all(x):
    n_a, n_b = 8, 16
    rows_a = x.shape[0] // n_a
    rows_b = rows_a // n_b
    vmem = pl.BlockSpec(memory_space=pltpu.VMEM)
    dma = pltpu.SemaphoreType.DMA
    return pl.pallas_call(
        reduce_kernel,
        out_shape=jax.ShapeDtypeStruct(x.shape, F32),
        in_specs=[vmem],
        out_specs=vmem,
        scratch_shapes=[
            pltpu.VMEM((n_a - 1, rows_a, 256), F32),
            pltpu.VMEM((rows_a, 256), F32),
            pltpu.VMEM((n_b - 1, rows_b, 256), F32),
            pltpu.VMEM((rows_a, 256), F32),
            dma((n_a - 1,)), dma((n_a - 1,)), dma((n_b - 1,)), dma((n_b - 1,)),
            dma((n_b - 1,)), dma((n_b - 1,)), dma((n_a - 1,)), dma((n_a - 1,)),
        ],
        compiler_params=pltpu.CompilerParams(
            collective_id=1, has_side_effects=True, vmem_limit_bytes=VMEM_LIMIT
        ),
        name="reduce",
    )(x)


def mm(a, b):
    return jnp.dot(a, b, precision=HIGH, preferred_element_type=F32)


def sweep_inverse(mats):
    n = mats[0].shape[0]
    row_at = lax.broadcasted_iota(jnp.int32, (n, n), 0)
    col_at = lax.broadcasted_iota(jnp.int32, (n, n), 1)
    mats = list(mats)
    for k in range(n):
        for i, m in enumerate(mats):
            row = m[k : k + 1, :]
            col = m[:, k : k + 1]
            inv = 1.0 / m[k : k + 1, k : k + 1]
            scaled = row * inv
            new = m - col * scaled
            new = jnp.where(row_at == k, scaled, new)
            new = jnp.where(col_at == k, jnp.where(row_at == k, -inv, col * inv), new)
            mats[i] = new
    return [-m for m in mats]


def spd_inverse(mats):
    h = mats[0].shape[0] // 2
    top = sweep_inverse([m[:h, :h] for m in mats])
    left = [mm(m[h:, :h], t) for m, t in zip(mats, top)]
    schur = sweep_inverse([m[h:, h:] - mm(l, m[:h, h:]) for m, l in zip(mats, left)])
    result = []
    for t, l, s in zip(top, left, schur):
        sl = mm(s, l)
        upper = jnp.concatenate([t + mm(l.T, sl), -sl.T], axis=1)
        lower = jnp.concatenate([-sl, s], axis=1)
        result.append(jnp.concatenate([upper, lower], axis=0))
    return result


def solve(matrix, inverse, rhs):
    x = mm(inverse, rhs)
    return x + mm(inverse, rhs - mm(matrix, x))


def algebra_kernel(grams, cd):
    rr0, g01, g11, g12 = (grams[i * 256 : (i + 1) * 256, :] for i in range(4))
    inv0, inv1 = spd_inverse([rr0, g01])
    a1 = solve(g01, inv1, rr0)
    ga = mm(g01, a1)
    g11a = mm(g11, a1)
    rr1 = rr0 - ga - ga.T + mm(a1.T, g11a)
    rr1 = 0.5 * (rr1 + rr1.T)
    b1 = solve(rr0, inv0, rr1)
    eye = jnp.where(
        lax.broadcasted_iota(jnp.int32, (256, 256), 0) == lax.broadcasted_iota(jnp.int32, (256, 256), 1), 1.0, 0.0
    )
    t = eye + b1
    cross = mm(t.T, g11a)
    pq2 = mm(t.T, mm(g01, t)) - cross - cross.T + mm(a1.T, mm(g12, a1))
    pq2 = 0.5 * (pq2 + pq2.T)
    (inv2,) = spd_inverse([pq2])
    a2 = solve(pq2, inv2, rr1)
    c = a1 + mm(t, a2)
    d = mm(a1, a2)
    cd[0], cd[1] = split(c)
    cd[2], cd[3] = split(d)


def algebra(grams):
    vmem = pl.BlockSpec(memory_space=pltpu.VMEM)
    return pl.pallas_call(
        algebra_kernel,
        out_shape=jax.ShapeDtypeStruct((4, 256, 256), BF16),
        in_specs=[vmem],
        out_specs=vmem,
        compiler_params=pltpu.CompilerParams(vmem_limit_bytes=VMEM_LIMIT),
        name="algebra",
    )(grams)


def final_kernel(cd, r0, q1, s, sol, res):
    c_hi, c_lo, d_hi, d_lo = cd[0], cd[1], cd[2], cd[3]
    r_hi, r_lo = split(r0[...])
    q_hi, q_lo = split(q1[...])
    s_hi, s_lo = split(s[...])

    def three(hi, lo, w_hi, w_lo):
        return dot(hi, w_hi) + (dot(hi, w_lo) + dot(lo, w_hi))

    sol[...] = three(r_hi, r_lo, c_hi, c_lo) - three(q_hi, q_lo, d_hi, d_lo)
    res[...] = r0[...] - three(q_hi, q_lo, c_hi, c_lo) + three(s_hi, s_lo, d_hi, d_lo)


def final(cd, r0, q1, s):
    rows = r0.shape[0]
    tile = 512
    spec = pl.BlockSpec((tile, 256), lambda i: (i, 0))
    return pl.pallas_call(
        final_kernel,
        grid=(rows // tile,),
        out_shape=(jax.ShapeDtypeStruct(r0.shape, F32),) * 2,
        in_specs=[pl.BlockSpec((4, 256, 256), lambda i: (0, 0, 0)), spec, spec, spec],
        out_specs=(spec, spec),
        compiler_params=pltpu.CompilerParams(vmem_limit_bytes=VMEM_LIMIT),
        name="final",
    )(cd, r0, q1, s)


def body(loads, pore_diag, near_blocks, near_cols, short_blocks, short_rows, short_cols):
    rows, cases = loads.shape
    brows = rows // 128
    plan, tile = make_plan(near_cols, short_rows, short_cols)
    scols = jnp.concatenate([short_rows.reshape(-1), short_cols.reshape(-1), near_cols])
    diag = pore_diag.reshape(brows, 128)
    short = short_blocks.reshape(-1, 128, 128)
    field = loads.reshape(brows, 128, cases)
    q1, g1 = apply(plan, scols, field, diag, near_blocks, short, tile)
    s, g2 = apply(plan, scols, q1, diag, near_blocks, short, tile)
    grams = reduce_all(jnp.concatenate([g1, g2], axis=0).reshape(4 * 256, 256))
    cd = algebra(grams)
    return final(cd, loads, q1.reshape(rows, cases), s.reshape(rows, cases))


def solution(mesh):
    in_specs = (
        P(("blk", "grp"), None),
        P(("blk", "grp")),
        P(("blk", "grp"), None, None),
        P(("blk", "grp")),
        P(("blk", "grp"), None, None, None),
        P(("blk", "grp"), None),
        P(("blk", "grp"), None),
    )
    out_specs = (P(("blk", "grp"), None), P(("blk", "grp"), None))
    return jax.shard_map(body, mesh=mesh, in_specs=in_specs, out_specs=out_specs, check_vma=False)
```

```python
import jax
import jax.numpy as jnp
from jax import lax
from jax.experimental import pallas as pl
from jax.experimental.pallas import tpu as pltpu
from jax.sharding import PartitionSpec as P

NEAR_PER = 3
HB = 4
SHORT = 2
N_BLK = 4
MESH = pl.DeviceIdType.MESH
HIGHEST = lax.Precision.HIGHEST
F32 = jnp.float32
BF16 = jnp.bfloat16
VMEM_LIMIT = 60 * 1024 * 1024

PERM, KEEP, LAST, SPERM, SKEEP, SLAST = range(6)


def split(x):
    hi = x.astype(BF16)
    lo = (x - hi.astype(F32)).astype(BF16)
    return hi, lo


def dot(a, b):
    return jnp.dot(a, b, preferred_element_type=F32)


def dot_t(a, b):
    return lax.dot_general(a, b, (((0,), (0,)), ((), ())), preferred_element_type=F32)


def three(w, e):
    hi, lo = split(w)
    return dot(jnp.concatenate([hi, hi, lo], axis=1), jnp.concatenate([e, e[:128]], axis=0))


def order(keys, n):
    square = (128, 128)
    at_col = lax.broadcasted_iota(jnp.int32, square, 0)
    at_row = lax.broadcasted_iota(jnp.int32, square, 1)
    lane = lax.broadcasted_iota(jnp.int32, (1, 128), 1)
    key = jnp.where(lane < n, keys, 64)
    both = key * 128 + lane
    key_col = jnp.broadcast_to(key, square).T
    both_col = jnp.broadcast_to(both, square).T

    def count(cond):
        return jnp.sum(jnp.where(cond, 1, 0), axis=0, keepdims=True)

    rank = count(both_col < jnp.broadcast_to(both, square))
    hit = jnp.broadcast_to(rank, square).T == at_row
    perm = jnp.sum(jnp.where(hit, at_col, 0), axis=0, keepdims=True)
    placed = jnp.sum(jnp.where(hit, key_col, 0), axis=0, keepdims=True)
    keep = jnp.where(count(key_col < jnp.broadcast_to(placed, square)) < lane, 1, 0)
    begin, end = count(key_col < at_row), count(key_col <= at_row)
    return perm, keep, jnp.where(end > begin, end, 0)


def lanes(values):
    lane = lax.broadcasted_iota(jnp.int32, (1, 128), 1)
    row = jnp.zeros((1, 128), jnp.int32)
    for i, value in enumerate(values):
        row = jnp.where(lane == i, value, row)
    return row


def krylov_kernel(
    cols, srows, scols, cols_row, field, diag, near, short,
    image, image2, grams1, grams2,
    f0, f1, ext, wn, ws, dsp, seg, rseg, tseg, halo, rim_out, rim_in, trm_out, trm_0, trm_1, fet_out, fet_0, fet_1,
    tile, idx_in, idx_sm, keyrow, plan_v, plan, tplan_v, tplan, acc_h, acc_l, acc_y,
    x1, buf1, part1, zbuf1, mid1, x2, buf2, part2, zbuf2, mid2,
    load_sem, out_sem, idx_sem, idx_send, idx_recv, halo_send, halo_recv, trm_send, trm_recv,
    fet_send, fet_recv, rim_send, rim_recv, red1_sem, zred1_sem, red2_sem, zred2_sem,
):
    brows = f0.shape[0]
    b = lax.axis_index("blk")
    g = lax.axis_index("grp")
    n_grp = lax.axis_size("grp")
    left = (b, lax.rem(g + n_grp - 1, n_grp))
    right = (b, lax.rem(g + 1, n_grp))
    peers = [None] + [(lax.rem(b + d, N_BLK), g) for d in range(1, N_BLK)]

    loads = [
        pltpu.make_async_copy(field, f0, load_sem.at[0]),
        pltpu.make_async_copy(short, ws, load_sem.at[1]),
        pltpu.make_async_copy(near, wn, load_sem.at[2]),
    ]
    for copy in loads:
        copy.start()

    barrier = pltpu.get_barrier_semaphore()

    def greet(i, c):
        peer = (b, lax.rem(g + i, n_grp))
        pl.semaphore_signal(barrier, inc=1, device_id=peer, device_id_type=MESH)
        return c

    lax.fori_loop(1, n_grp, greet, 0)
    for peer in peers[1:]:
        pl.semaphore_signal(barrier, inc=1, device_id=peer, device_id_type=MESH)

    def remote(src, dst, send, recv, peer):
        copy = pltpu.make_async_remote_copy(
            src_ref=src, dst_ref=dst, send_sem=send, recv_sem=recv,
            device_id=peer, device_id_type=MESH,
        )
        copy.start()
        return copy

    sub = lax.broadcasted_iota(jnp.int32, (8, 128), 0)
    lane = lax.broadcasted_iota(jnp.int32, (8, 128), 1)
    own = jnp.zeros((8, 128), jnp.int32)
    for c in range(N_BLK):
        for s in range(SHORT):
            own = jnp.where((sub == c) & (lane == s), scols[c, s], own)
    tile[...] = own
    pl.semaphore_wait(barrier, n_grp - 1 + N_BLK - 1)
    idx_copies = [
        remote(tile, idx_in.at[3 - d], idx_send.at[d - 1], idx_recv.at[3 - d], peers[d])
        for d in range(1, N_BLK)
    ]
    keyrow[...] = jnp.zeros(keyrow.shape, jnp.int32)
    keyrow[0:1, :96] = cols_row[...]
    plan_v[...] = jnp.zeros(plan_v.shape, jnp.int32)
    plan_v[0:1, :], plan_v[1:2, :], plan_v[2:3, :] = order(keyrow[0:1, :], 96)
    plan_v[3:4, :], plan_v[4:5, :], plan_v[5:6, :] = order(
        lanes([srows[c, s] for c in range(N_BLK) for s in range(SHORT)]), 8
    )
    plan_copy = pltpu.make_async_copy(plan_v, plan, idx_sem.at[0])
    plan_copy.start()

    def spread_diag(r, c):
        dsp[r] = jnp.broadcast_to(diag[pl.ds(r, 1), :], (128, 128)).T * 0.5
        return c

    lax.fori_loop(0, brows, spread_diag, 0)
    seg[0] = jnp.zeros(seg.shape[1:], F32)
    rseg[0] = jnp.zeros(rseg.shape[1:], F32)
    tseg[0] = jnp.zeros(tseg.shape[1:], F32)
    for copy in idx_copies:
        copy.wait()
    idx_copy = pltpu.make_async_copy(idx_in, idx_sm, idx_sem.at[1])
    idx_copy.start()
    idx_copy.wait()
    tplan_v[...] = jnp.zeros(tplan_v.shape, jnp.int32)
    wanted = [scols[b, s] for s in range(SHORT)]
    for d in range(1, N_BLK):
        wanted += [idx_sm[d - 1, b, s] for s in range(SHORT)]
    tplan_v[0:1, :], tplan_v[1:2, :], tplan_v[2:3, :] = order(lanes(wanted), 8)
    tplan_copy = pltpu.make_async_copy(tplan_v, tplan, idx_sem.at[2])
    tplan_copy.start()
    plan_copy.wait()
    tplan_copy.wait()

    class Reduce:
        def __init__(self, x, buf, part, zbuf, mid, res, sems, zsems):
            self.x, self.buf, self.part, self.zbuf, self.mid, self.res = x, buf, part, zbuf, mid, res
            self.sems, self.zsems = sems, zsems
            self.rows = x.shape[0] // n_grp

        def piece(self, ref, at):
            return ref.at[pl.ds(pl.multiple_of(at * self.rows, self.rows), self.rows)]

        def each(self, act):
            def step(i, c):
                act(i)
                return c

            lax.fori_loop(1, n_grp, step, 0)

        def spread(self, i):
            t = lax.rem(g + i, n_grp)
            return pltpu.make_async_remote_copy(
                src_ref=self.piece(self.x, t), dst_ref=self.buf.at[n_grp - 1 - i],
                send_sem=self.sems.at[0, i - 1], recv_sem=self.sems.at[1, n_grp - 1 - i],
                device_id=(b, t), device_id_type=MESH,
            )

        def share(self, i):
            t = lax.rem(g + i, n_grp)
            return pltpu.make_async_remote_copy(
                src_ref=self.mid, dst_ref=self.piece(self.res, g),
                send_sem=self.sems.at[2, i - 1], recv_sem=self.sems.at[3, n_grp - 1 - i],
                device_id=(b, t), device_id_type=MESH,
            )

        def scatter(self):
            self.each(lambda i: self.spread(i).start())

        def across(self):
            self.each(lambda i: self.spread(i).wait())
            total = self.x[pl.ds(pl.multiple_of(g * self.rows, self.rows), self.rows)]
            for i in range(n_grp - 1):
                total += self.buf[i]
            self.part[...] = total
            self.copies = [
                remote(self.part, self.zbuf.at[3 - d], self.zsems.at[0, d - 1], self.zsems.at[1, 3 - d], peers[d])
                for d in range(1, N_BLK)
            ]

        def gather(self):
            for copy in self.copies:
                copy.wait()
            total = jnp.zeros(self.part.shape, F32)
            for z in range(N_BLK):
                term = jnp.where(b == z, 1.0, 0.0) * self.part[...]
                for d in range(1, N_BLK):
                    term += jnp.where(lax.rem(b + d, N_BLK) == z, 1.0, 0.0) * self.zbuf[d - 1]
                total += term
            self.mid[...] = total
            self.res[pl.ds(pl.multiple_of(g * self.rows, self.rows), self.rows)] = total
            self.each(lambda i: self.share(i).start())

        def finish(self):
            self.each(lambda i: self.share(i).wait())

    reduce1 = Reduce(x1, buf1, part1, zbuf1, mid1, grams1, red1_sem, zred1_sem)
    reduce2 = Reduce(x2, buf2, part2, zbuf2, mid2, grams2, red2_sem, zred2_sem)

    per = 8
    back = 12
    rows_at_once = 8

    def operate(stage, fv, out, x_h, x_y, x_at, trm, fet):
        if stage == 0:
            loads[0].wait()
        halo_copies = [
            remote(fv.at[pl.ds(0, HB)], halo.at[stage, pl.ds(HB, HB)],
                   halo_send.at[stage, 0], halo_recv.at[stage, 0], left),
            remote(fv.at[pl.ds(brows - HB, HB)], halo.at[stage, pl.ds(0, HB)],
                   halo_send.at[stage, 1], halo_recv.at[stage, 1], right),
        ]

        for d in range(N_BLK):
            for s in range(SHORT):
                if d == 0:
                    fet[s] = fv[wanted[s]]
                else:
                    fet_out[(d - 1) * SHORT + s] = fv[wanted[d * SHORT + s]]
        fet_copies = [
            remote(fet_out.at[pl.ds((d - 1) * SHORT, SHORT)], fet.at[pl.ds((4 - d) * SHORT, SHORT)],
                   fet_send.at[stage, d - 1], fet_recv.at[stage, 3 - d], peers[d])
            for d in (1, 3, 2)
        ]

        def split_own(i, c):
            for u in range(4):
                r = i * 4 + u
                hi, lo = split(fv[r])
                ext[HB + r, :128, :] = hi
                ext[HB + r, 128:, :] = lo
            return c

        lax.fori_loop(0, brows // 4, split_own, 0)

        if stage == 0:
            loads[1].wait()
        terms = []
        for d in range(N_BLK):
            c = lax.rem(b + d, N_BLK)
            for s in range(SHORT):
                terms.append(three(ws[c * SHORT + s].T, ext[HB + srows[c, s]]))
        for s in range(SHORT):
            trm[s] = terms[s]
        for i in range(SHORT, N_BLK * SHORT):
            trm_out[i - SHORT] = terms[i]
        trm_copies = [
            remote(trm_out.at[pl.ds((d - 1) * SHORT, SHORT)], trm.at[pl.ds((4 - d) * SHORT, SHORT)],
                   trm_send.at[stage, d - 1], trm_recv.at[stage, 3 - d], peers[d])
            for d in (1, 3, 2)
        ]

        if stage == 0:
            loads[2].wait()

        def backward(i, carry):
            terms = []
            for u in range(back):
                m = plan[PERM, i * back + u]
                terms.append(three(wn[m].T, ext[HB + lax.div(m, NEAR_PER)]))
            run = seg[i * back]
            for u in range(back):
                run = run * plan[KEEP, i * back + u].astype(F32) + terms[u]
                seg[i * back + u + 1] = run
            return carry

        lax.fori_loop(0, brows * NEAR_PER // back, backward, 0)
        for q in range(HB):
            rim_out[q] = seg[plan[LAST, q]]
            rim_out[HB + q] = seg[plan[LAST, HB + brows + q]]
        rim_copies = [
            remote(rim_out.at[pl.ds(0, HB)], rim_in.at[stage, pl.ds(HB, HB)],
                   rim_send.at[stage, 0], rim_recv.at[stage, 0], left),
            remote(rim_out.at[pl.ds(HB, HB)], rim_in.at[stage, pl.ds(0, HB)],
                   rim_send.at[stage, 1], rim_recv.at[stage, 1], right),
        ]

        acc_h[...] = jnp.zeros(acc_h.shape, F32)
        acc_l[...] = jnp.zeros(acc_l.shape, F32)
        acc_y[...] = jnp.zeros(acc_y.shape, F32)

        def halves(i):
            hi = ext[pl.ds(HB + i * per, per), :128, :].reshape(per * 128, 256)
            lo = ext[pl.ds(HB + i * per, per), 128:, :].reshape(per * 128, 256)
            return hi, lo

        def gram(i, c):
            hi, lo = halves(i)
            both = dot_t(hi, jnp.concatenate([hi, lo], axis=1))
            acc_h[...] += both[:, :256] + dot_t(lo, lo)
            acc_l[...] += both[:, 256:]
            return c

        lax.fori_loop(0, brows // per, gram, 0)
        low = acc_l[...]
        x_h[pl.ds(x_at, 256)] = acc_h[...] + (low + low.T)
        if stage == 1:
            reduce1.scatter()

        for copy in halo_copies:
            copy.wait()
        for q in range(2 * HB):
            hi, lo = split(halo[stage, q])
            at = q if q < HB else q + brows
            ext[at, :128, :] = hi
            ext[at, 128:, :] = lo

        def half_diag(r):
            d = dsp[r]
            return jnp.concatenate([d, d], axis=1) * fv[r]

        def forward(i, c):
            sums = []
            for u in range(rows_at_once):
                lhs, rhs = [], []
                for j in range(NEAR_PER):
                    m = (i * rows_at_once + u) * NEAR_PER + j
                    hi, lo = split(wn[m])
                    e = ext[cols[m]]
                    lhs += [hi, hi, lo]
                    rhs += [e, e[:128]]
                sums.append(dot(jnp.concatenate(lhs, axis=1), jnp.concatenate(rhs, axis=0)))
            for u in range(rows_at_once):
                r = i * rows_at_once + u
                out[r] = half_diag(r) + sums[u]
            return c

        lax.fori_loop(0, brows // rows_at_once, forward, 0)
        if stage == 1:
            reduce1.across()

        for copy in fet_copies:
            copy.wait()
        terms = []
        for i in range(N_BLK * SHORT):
            n = plan[SPERM, i]
            slot = lax.rem(lax.div(n, SHORT) + N_BLK - b, N_BLK) * SHORT + lax.rem(n, SHORT)
            hi, lo = split(fet[slot])
            terms.append(three(ws[n], jnp.concatenate([hi, lo], axis=0)))
        run = rseg[0]
        for i in range(N_BLK * SHORT):
            run = run * plan[SKEEP, i].astype(F32) + terms[i]
            rseg[i + 1] = run

        def gram_y(i, c):
            parts = []
            for u in range(per):
                r = i * per + u
                f = out[r] + rseg[plan[SLAST, r]]
                out[r] = f
                parts.append(f)
            fh, fl = split(jnp.concatenate(parts, axis=0))
            hi, lo = halves(i)
            both = dot_t(hi, jnp.concatenate([fh, fl], axis=1))
            acc_y[...] += (both[:, :256] + both[:, 256:]) + dot_t(lo, fh)
            return c

        lax.fori_loop(0, brows // per, gram_y, 0)
        y = acc_y[...]
        x_y[pl.ds(256 if stage == 0 else 0, 256)] = y + y.T
        if stage == 1:
            reduce2.scatter()
            reduce1.gather()

        for copy in trm_copies:
            copy.wait()
        run = tseg[0]
        for i in range(N_BLK * SHORT):
            run = run * tplan[KEEP, i].astype(F32) + trm[tplan[PERM, i]]
            tseg[i + 1] = run

        def finish(i, c):
            for u in range(4):
                r = i * 4 + u
                out[r] = (out[r] + half_diag(r)) + (seg[plan[LAST, HB + r]] + tseg[tplan[LAST, r]])
            return c

        if stage == 1:
            reduce2.across()
        lax.fori_loop(0, brows // 4, finish, 0)
        if stage == 1:
            reduce2.gather()
        for copy in rim_copies:
            copy.wait()
        for q in range(HB):
            out[q] = out[q] + rim_in[stage, q]
            out[brows - HB + q] = out[brows - HB + q] + rim_in[stage, HB + q]

    operate(0, f0, f1, x1, x1, 0, trm_0, fet_0)
    copy1 = pltpu.make_async_copy(f1, image, out_sem.at[0])
    copy1.start()
    operate(1, f1, f0, x1, x2, 512, trm_1, fet_1)
    copy2 = pltpu.make_async_copy(f0, image2, out_sem.at[1])
    copy2.start()
    reduce1.finish()
    reduce2.finish()
    copy1.wait()
    copy2.wait()


def krylov(near_cols, short_rows, short_cols, field, diag, near, short):
    brows = field.shape[0]
    smem = pl.BlockSpec(memory_space=pltpu.SMEM)
    vmem = pl.BlockSpec(memory_space=pltpu.VMEM)
    hbm = pl.BlockSpec(memory_space=pl.ANY)
    n_grp = 32
    dma = pltpu.SemaphoreType.DMA

    def block(*n):
        return pltpu.VMEM(n + (128, 256), F32)

    def words(*n):
        return pltpu.VMEM(n + (8, 128), jnp.int32)

    def reduce_scratch(rows):
        piece = rows // n_grp
        return [
            pltpu.VMEM((rows, 256), F32), pltpu.VMEM((n_grp - 1, piece, 256), F32), pltpu.VMEM((piece, 256), F32),
            pltpu.VMEM((N_BLK - 1, piece, 256), F32), pltpu.VMEM((piece, 256), F32),
        ]

    return pl.pallas_call(
        krylov_kernel,
        out_shape=(
            jax.ShapeDtypeStruct(field.shape, F32),
            jax.ShapeDtypeStruct(field.shape, F32),
            jax.ShapeDtypeStruct((768, 256), F32),
            jax.ShapeDtypeStruct((256, 256), F32),
        ),
        in_specs=[smem, smem, smem, vmem, hbm, vmem, hbm, hbm],
        out_specs=(hbm, hbm, vmem, vmem),
        scratch_shapes=[
            block(brows), block(brows),
            pltpu.VMEM((brows + 2 * HB, 256, 256), BF16),
            pltpu.VMEM(near.shape, F32),
            pltpu.VMEM(short.shape, F32),
            pltpu.VMEM((brows, 128, 128), F32),
            block(brows * NEAR_PER + 1), block(9), block(9),
            block(2, 2 * HB), block(2 * HB), block(2, 2 * HB),
            block(6), block(8), block(8), block(6), block(8), block(8),
            words(), words(3), pltpu.SMEM((3, 8, 128), jnp.int32), words(),
            words(), pltpu.SMEM((8, 128), jnp.int32), words(), pltpu.SMEM((8, 128), jnp.int32),
            pltpu.VMEM((256, 256), F32), pltpu.VMEM((256, 256), F32), pltpu.VMEM((256, 256), F32),
            *reduce_scratch(768), *reduce_scratch(256),
            dma((3,)), dma((2,)), dma((3,)), dma((3,)), dma((3,)),
            dma((2, 2)), dma((2, 2)), dma((2, 3)), dma((2, 3)), dma((2, 3)), dma((2, 3)),
            dma((2, 2)), dma((2, 2)),
            dma((4, n_grp - 1)), dma((2, 3)), dma((4, n_grp - 1)), dma((2, 3)),
        ],
        compiler_params=pltpu.CompilerParams(
            collective_id=0, has_side_effects=True, vmem_limit_bytes=VMEM_LIMIT
        ),
        name="krylov",
    )(near_cols, short_rows, short_cols, near_cols.reshape(1, -1), field, diag, near, short)


def mm(a, b):
    return jnp.dot(a, b, precision=HIGHEST, preferred_element_type=F32)


def tail_kernel(
    grams1, grams2, r0, q1, s2, sol, res,
    rv, qv, sv, sol_v, res_v, w_sol, w_res, inv, err, load_sem, sol_sem, res_sem,
):
    loads = [
        pltpu.make_async_copy(src, dst, load_sem.at[i])
        for i, (src, dst) in enumerate(((r0, rv), (q1, qv), (s2, sv)))
    ]
    for copy in loads:
        copy.start()
    n = 256
    diagonal = lax.broadcasted_iota(jnp.int32, (n, n), 0) == lax.broadcasted_iota(jnp.int32, (n, n), 1)
    eye = jnp.where(diagonal, 1.0, 0.0)

    def scales(m):
        kept = jnp.where(diagonal, m, 0.0)
        return lax.rsqrt(jnp.sum(kept, axis=0, keepdims=True)), lax.rsqrt(jnp.sum(kept, axis=1, keepdims=True))

    def size(m):
        return jnp.max(jnp.abs(m))

    def square(limit):
        def step(state):
            e, x = err[...], inv[...]
            inv[...] = x + mm(x, e)
            e = mm(e, e)
            err[...] = e
            return state[0] + 1, size(e)

        return lax.while_loop(
            lambda state: (state[0] < limit) & (state[1] > 1e-5), step, (jnp.int32(0), size(err[...]))
        )[1]

    def polish(m):
        def step(state):
            x = inv[...]
            e = eye - mm(m, x)
            inv[...] = x + mm(x, e)
            return state[0] + 1, size(e)

        lax.while_loop(lambda state: (state[0] < 6) & (state[1] > 1e-5), step, (jnp.int32(0), F32(1.0)))

    def spd_inverse(m, guess):
        along, down = scales(m)
        scaled = m * along * down

        def from_norm():
            bound = jnp.max(jnp.sum(jnp.abs(scaled), axis=1, keepdims=True))
            start = eye / bound
            inv[...] = start
            err[...] = eye - scaled / bound
            square(48)

        if guess is None:
            from_norm()
        else:
            near = guess / along / down
            z = mm(scaled, near)
            tau = n / jnp.sum(jnp.where(diagonal, z, 0.0))
            inv[...] = near * tau
            err[...] = eye - z * tau
            left = square(6)

            @pl.when(jnp.logical_not(left <= 1e-5))
            def _():
                from_norm()

        polish(scaled)
        return inv[...] * along * down

    def solve(matrix, inverse, rhs):
        x = mm(inverse, rhs)
        return x + mm(inverse, rhs - mm(matrix, x))

    rr0, g01, g11 = (grams1[i * n : (i + 1) * n, :] for i in range(3))
    g12 = grams2[...]
    inv0 = spd_inverse(rr0, None)
    a1 = solve(g01, spd_inverse(g01, inv0), rr0)
    ga = mm(g01, a1)
    g11a = mm(g11, a1)
    rr1 = (rr0 - ga) + (mm(a1.T, g11a) - ga.T)
    rr1 = 0.5 * (rr1 + rr1.T)
    t = eye + solve(rr0, inv0, rr1)
    cross = mm(t.T, g11a)
    pq2 = (mm(t.T, mm(g01, t)) - cross) + (mm(a1.T, mm(g12, a1)) - cross.T)
    pq2 = 0.5 * (pq2 + pq2.T)
    a2 = solve(pq2, spd_inverse(pq2, inv0), rr1)
    c_hi, c_lo = split(a1 + mm(t, a2))
    d_hi, d_lo = split(mm(a1, a2))
    for i, part in enumerate((c_hi, c_lo, c_hi, -d_hi, -d_lo, -d_hi)):
        w_sol[i * n : (i + 1) * n, :] = part
        w_res[i * n : (i + 1) * n, :] = -part

    for copy in loads:
        copy.wait()
    tile = 512
    tiles = rv.shape[0] // tile

    def three(x, y):
        x_hi, x_lo = split(x)
        y_hi, y_lo = split(y)
        return jnp.concatenate([x_hi, x_hi, x_lo, y_hi, y_hi, y_lo], axis=1)

    for i in range(tiles):
        at = pl.ds(i * tile, tile)
        sol_v[at] = dot(three(rv[at], qv[at]), w_sol[...])
        pltpu.make_async_copy(sol_v.at[at], sol.at[at], sol_sem.at[i]).start()
        res_v[at] = rv[at] + dot(three(qv[at], sv[at]), w_res[...])
        pltpu.make_async_copy(res_v.at[at], res.at[at], res_sem.at[i]).start()
    for i in range(tiles):
        at = pl.ds(i * tile, tile)
        pltpu.make_async_copy(sol_v.at[at], sol.at[at], sol_sem.at[i]).wait()
        pltpu.make_async_copy(res_v.at[at], res.at[at], res_sem.at[i]).wait()


def tail(grams1, grams2, r0, q1, s2):
    vmem = pl.BlockSpec(memory_space=pltpu.VMEM)
    hbm = pl.BlockSpec(memory_space=pl.ANY)
    dma = pltpu.SemaphoreType.DMA
    field = pltpu.VMEM(r0.shape, F32)
    return pl.pallas_call(
        tail_kernel,
        out_shape=(jax.ShapeDtypeStruct(r0.shape, F32),) * 2,
        in_specs=[vmem, vmem, hbm, hbm, hbm],
        out_specs=(hbm, hbm),
        scratch_shapes=[
            field, field, field, field, field,
            pltpu.VMEM((1536, 256), BF16), pltpu.VMEM((1536, 256), BF16),
            pltpu.VMEM((256, 256), F32), pltpu.VMEM((256, 256), F32),
            dma((3,)), dma((8,)), dma((8,)),
        ],
        compiler_params=pltpu.CompilerParams(vmem_limit_bytes=VMEM_LIMIT),
        name="tail",
    )(grams1, grams2, r0, q1, s2)


def body(loads, pore_diag, near_blocks, near_cols, short_blocks, short_rows, short_cols):
    rows, cases = loads.shape
    brows = rows // 128
    q1, s2, grams1, grams2 = krylov(
        near_cols, short_rows, short_cols, loads.reshape(brows, 128, cases), pore_diag.reshape(brows, 128),
        near_blocks, short_blocks.reshape(-1, 128, 128),
    )
    return tail(grams1, grams2, loads, q1.reshape(rows, cases), s2.reshape(rows, cases))


def solution(mesh):
    in_specs = (
        P(("blk", "grp"), None),
        P(("blk", "grp")),
        P(("blk", "grp"), None, None),
        P(("blk", "grp")),
        P(("blk", "grp"), None, None, None),
        P(("blk", "grp"), None),
        P(("blk", "grp"), None),
    )
    out_specs = (P(("blk", "grp"), None), P(("blk", "grp"), None))
    return jax.shard_map(body, mesh=mesh, in_specs=in_specs, out_specs=out_specs, check_vma=False)
```

```python
import jax
import jax.numpy as jnp
from jax import lax
from jax.experimental import pallas as pl
from jax.experimental.pallas import tpu as pltpu
from jax.sharding import PartitionSpec as P

NEAR_PER = 3
HB = 4
SHORT = 2
N_BLK = 4
MESH = pl.DeviceIdType.MESH
HIGHEST = lax.Precision.HIGHEST
F32 = jnp.float32
BF16 = jnp.bfloat16
VMEM_LIMIT = 60 * 1024 * 1024

PERM, KEEP, LAST, SPERM, SKEEP, SLAST = range(6)


def split(x):
    hi = x.astype(BF16)
    lo = (x - hi.astype(F32)).astype(BF16)
    return hi, lo


def dot(a, b):
    return jnp.dot(a, b, preferred_element_type=F32)


def dot_t(a, b):
    return lax.dot_general(a, b, (((0,), (0,)), ((), ())), preferred_element_type=F32)


def three(w, e):
    hi, lo = split(w)
    return dot(jnp.concatenate([hi, hi, lo], axis=1), jnp.concatenate([e, e[:128]], axis=0))


def order(keys, n):
    square = (128, 128)
    at_col = lax.broadcasted_iota(jnp.int32, square, 0)
    at_row = lax.broadcasted_iota(jnp.int32, square, 1)
    lane = lax.broadcasted_iota(jnp.int32, (1, 128), 1)
    key = jnp.where(lane < n, keys, 64)
    both = key * 128 + lane
    key_col = jnp.broadcast_to(key, square).T
    both_col = jnp.broadcast_to(both, square).T

    def count(cond):
        return jnp.sum(jnp.where(cond, 1, 0), axis=0, keepdims=True)

    rank = count(both_col < jnp.broadcast_to(both, square))
    hit = jnp.broadcast_to(rank, square).T == at_row
    perm = jnp.sum(jnp.where(hit, at_col, 0), axis=0, keepdims=True)
    placed = jnp.sum(jnp.where(hit, key_col, 0), axis=0, keepdims=True)
    keep = jnp.where(count(key_col < jnp.broadcast_to(placed, square)) < lane, 1, 0)
    begin, end = count(key_col < at_row), count(key_col <= at_row)
    return perm, keep, jnp.where(end > begin, end, 0)


def lanes(values):
    lane = lax.broadcasted_iota(jnp.int32, (1, 128), 1)
    row = jnp.zeros((1, 128), jnp.int32)
    for i, value in enumerate(values):
        row = jnp.where(lane == i, value, row)
    return row


def krylov_kernel(
    cols, srows, scols, cols_row, field, diag, near, short,
    image, image2, grams1, grams2,
    f0, f1, ext, wn, ws, dsp, seg, rseg, tseg, halo, rim_out, rim_in, trm_out, trm_0, trm_1, fet_out, fet_0, fet_1,
    tile, idx_in, idx_sm, keyrow, plan_v, plan, tplan_v, tplan, acc_h, acc_l, acc_y,
    x1, pair1, half1, buf1, part1, zbuf1, mid1, x2, buf2, part2, zbuf2, mid2,
    load_sem, out_sem, idx_sem, idx_send, idx_recv, halo_send, halo_recv, trm_send, trm_recv,
    fet_send, fet_recv, rim_send, rim_recv, pair_sem, red1_sem, zred1_sem, red2_sem, zred2_sem,
):
    brows = f0.shape[0]
    b = lax.axis_index("blk")
    g = lax.axis_index("grp")
    n_grp = lax.axis_size("grp")
    left = (b, lax.rem(g + n_grp - 1, n_grp))
    right = (b, lax.rem(g + 1, n_grp))
    peers = [None] + [(lax.rem(b + d, N_BLK), g) for d in range(1, N_BLK)]

    loads = [
        pltpu.make_async_copy(field, f0, load_sem.at[0]),
        pltpu.make_async_copy(short, ws, load_sem.at[1]),
        pltpu.make_async_copy(near, wn, load_sem.at[2]),
    ]
    for copy in loads:
        copy.start()

    barrier = pltpu.get_barrier_semaphore()

    def greet(i, c):
        peer = (b, lax.rem(g + i, n_grp))
        pl.semaphore_signal(barrier, inc=1, device_id=peer, device_id_type=MESH)
        return c

    lax.fori_loop(1, n_grp, greet, 0)
    for peer in peers[1:]:
        pl.semaphore_signal(barrier, inc=1, device_id=peer, device_id_type=MESH)

    def remote(src, dst, send, recv, peer):
        copy = pltpu.make_async_remote_copy(
            src_ref=src, dst_ref=dst, send_sem=send, recv_sem=recv,
            device_id=peer, device_id_type=MESH,
        )
        copy.start()
        return copy

    sub = lax.broadcasted_iota(jnp.int32, (8, 128), 0)
    lane = lax.broadcasted_iota(jnp.int32, (8, 128), 1)
    own = jnp.zeros((8, 128), jnp.int32)
    for c in range(N_BLK):
        for s in range(SHORT):
            own = jnp.where((sub == c) & (lane == s), scols[c, s], own)
    tile[...] = own
    pl.semaphore_wait(barrier, n_grp - 1 + N_BLK - 1)
    idx_copies = [
        remote(tile, idx_in.at[3 - d], idx_send.at[d - 1], idx_recv.at[3 - d], peers[d])
        for d in range(1, N_BLK)
    ]
    for copy in idx_copies:
        copy.wait()
    idx_copy = pltpu.make_async_copy(idx_in, idx_sm, idx_sem.at[1])
    idx_copy.start()
    idx_copy.wait()
    wanted = [scols[b, s] for s in range(SHORT)]
    for d in range(1, N_BLK):
        wanted += [idx_sm[d - 1, b, s] for s in range(SHORT)]
    def sector_sum(part, zbuf):
        total = jnp.zeros(part.shape, F32)
        for z in range(N_BLK):
            term = jnp.where(b == z, 1.0, 0.0) * part[...]
            for d in range(1, N_BLK):
                term += jnp.where(lax.rem(b + d, N_BLK) == z, 1.0, 0.0) * zbuf[d - 1]
            total += term
        return total

    class Reduce:
        def __init__(self, x, buf, part, zbuf, mid, res, sems, zsems):
            self.x, self.buf, self.part, self.zbuf, self.mid, self.res = x, buf, part, zbuf, mid, res
            self.sems, self.zsems = sems, zsems
            self.rows = x.shape[0] // n_grp

        def piece(self, ref, at):
            return ref.at[pl.ds(pl.multiple_of(at * self.rows, self.rows), self.rows)]

        def each(self, act):
            def step(i, c):
                act(i)
                return c

            lax.fori_loop(1, n_grp, step, 0)

        def spread(self, i):
            t = lax.rem(g + i, n_grp)
            return pltpu.make_async_remote_copy(
                src_ref=self.piece(self.x, t), dst_ref=self.buf.at[n_grp - 1 - i],
                send_sem=self.sems.at[0, i - 1], recv_sem=self.sems.at[1, n_grp - 1 - i],
                device_id=(b, t), device_id_type=MESH,
            )

        def share(self, i):
            t = lax.rem(g + i, n_grp)
            return pltpu.make_async_remote_copy(
                src_ref=self.mid, dst_ref=self.piece(self.res, g),
                send_sem=self.sems.at[2, i - 1], recv_sem=self.sems.at[3, n_grp - 1 - i],
                device_id=(b, t), device_id_type=MESH,
            )

        def scatter(self):
            self.each(lambda i: self.spread(i).start())

        def across(self):
            self.each(lambda i: self.spread(i).wait())
            total = self.x[pl.ds(pl.multiple_of(g * self.rows, self.rows), self.rows)]
            for i in range(n_grp - 1):
                total += self.buf[i]
            self.part[...] = total
            self.copies = [
                remote(self.part, self.zbuf.at[3 - d], self.zsems.at[0, d - 1], self.zsems.at[1, 3 - d], peers[d])
                for d in range(1, N_BLK)
            ]

        def gather(self):
            for copy in self.copies:
                copy.wait()
            total = sector_sum(self.part, self.zbuf)
            self.mid[...] = total
            self.res[pl.ds(pl.multiple_of(g * self.rows, self.rows), self.rows)] = total
            self.each(lambda i: self.share(i).start())

        def finish(self):
            self.each(lambda i: self.share(i).wait())

    class PairReduce:
        def __init__(self, x, pair, half, buf, part, zbuf, mid, res, psems, sems, zsems):
            self.x, self.pair_in, self.half, self.buf = x, pair, half, buf
            self.part, self.zbuf, self.mid, self.res = part, zbuf, mid, res
            self.psems, self.sems, self.zsems = psems, sems, zsems
            self.core, self.plane, self.planes = lax.rem(g, 2), lax.div(g, 2), n_grp // 2
            self.other = (b, self.plane * 2 + 1 - self.core)
            self.half_rows = x.shape[0] // 2
            self.rows = self.half_rows // self.planes

        def halved(self, ref, core):
            return ref.at[pl.ds(pl.multiple_of(core * self.half_rows, self.half_rows), self.half_rows)]

        def each(self, act):
            def step(i, c):
                act(i)
                return c

            lax.fori_loop(1, self.planes, step, 0)

        def spread(self, i):
            t = lax.rem(self.plane + i, self.planes)
            return pltpu.make_async_remote_copy(
                src_ref=self.half.at[pl.ds(pl.multiple_of(t * self.rows, self.rows), self.rows)],
                dst_ref=self.buf.at[self.planes - 1 - i],
                send_sem=self.sems.at[0, i - 1], recv_sem=self.sems.at[1, self.planes - 1 - i],
                device_id=(b, t * 2 + self.core), device_id_type=MESH,
            )

        def own_piece(self):
            at = self.core * self.half_rows + self.plane * self.rows
            return pl.ds(pl.multiple_of(at, self.rows), self.rows)

        def share(self, i):
            t = lax.rem(self.plane + i, self.planes)
            return pltpu.make_async_remote_copy(
                src_ref=self.mid, dst_ref=self.res.at[self.own_piece()],
                send_sem=self.sems.at[2, i - 1], recv_sem=self.sems.at[3, self.planes - 1 - i],
                device_id=(b, t * 2 + self.core), device_id_type=MESH,
            )

        def pair(self):
            self.paired = remote(
                self.halved(self.x, 1 - self.core), self.pair_in, self.psems.at[0], self.psems.at[1], self.other
            )

        def scatter(self):
            self.paired.wait()
            at = pl.multiple_of(self.core * self.half_rows, self.half_rows)
            self.half[...] = self.x[pl.ds(at, self.half_rows)] + self.pair_in[...]
            self.each(lambda i: self.spread(i).start())

        def across(self):
            self.each(lambda i: self.spread(i).wait())
            total = self.half[pl.ds(pl.multiple_of(self.plane * self.rows, self.rows), self.rows)]
            for i in range(self.planes - 1):
                total += self.buf[i]
            self.part[...] = total
            self.copies = [
                remote(self.part, self.zbuf.at[3 - d], self.zsems.at[0, d - 1], self.zsems.at[1, 3 - d], peers[d])
                for d in range(1, N_BLK)
            ]

        def gather(self):
            for copy in self.copies:
                copy.wait()
            total = sector_sum(self.part, self.zbuf)
            self.mid[...] = total
            self.res[self.own_piece()] = total
            self.each(lambda i: self.share(i).start())

        def regroup(self):
            self.each(lambda i: self.share(i).wait())
            mine = self.halved(self.res, self.core)
            self.paired = remote(mine, mine, self.psems.at[2], self.psems.at[3], self.other)

        def finish(self):
            self.paired.wait()

    reduce1 = PairReduce(x1, pair1, half1, buf1, part1, zbuf1, mid1, grams1, pair_sem, red1_sem, zred1_sem)
    reduce2 = Reduce(x2, buf2, part2, zbuf2, mid2, grams2, red2_sem, zred2_sem)

    per = 8
    back = 12
    rows_at_once = 8

    def make_plan():
        keyrow[...] = jnp.zeros(keyrow.shape, jnp.int32)
        keyrow[0:1, :96] = cols_row[...]
        plan_v[...] = jnp.zeros(plan_v.shape, jnp.int32)
        plan_v[0:1, :], plan_v[1:2, :], plan_v[2:3, :] = order(keyrow[0:1, :], 96)
        plan_v[3:4, :], plan_v[4:5, :], plan_v[5:6, :] = order(
            lanes([srows[c, s] for c in range(N_BLK) for s in range(SHORT)]), 8
        )
        plan_copy = pltpu.make_async_copy(plan_v, plan, idx_sem.at[0])
        plan_copy.start()

        def spread_diag(r, c):
            dsp[r] = jnp.broadcast_to(diag[pl.ds(r, 1), :], (128, 128)).T * 0.5
            return c

        lax.fori_loop(0, brows, spread_diag, 0)
        seg[0] = jnp.zeros(seg.shape[1:], F32)
        rseg[0] = jnp.zeros(rseg.shape[1:], F32)
        tseg[0] = jnp.zeros(tseg.shape[1:], F32)
        tplan_v[...] = jnp.zeros(tplan_v.shape, jnp.int32)
        tplan_v[0:1, :], tplan_v[1:2, :], tplan_v[2:3, :] = order(lanes(wanted), 8)
        tplan_copy = pltpu.make_async_copy(tplan_v, tplan, idx_sem.at[2])
        tplan_copy.start()
        plan_copy.wait()
        tplan_copy.wait()

    def operate(stage, fv, out, x_h, x_y, x_at, trm, fet):
        if stage == 0:
            loads[0].wait()
        halo_copies = [
            remote(fv.at[pl.ds(0, HB)], halo.at[stage, pl.ds(HB, HB)],
                   halo_send.at[stage, 0], halo_recv.at[stage, 0], left),
            remote(fv.at[pl.ds(brows - HB, HB)], halo.at[stage, pl.ds(0, HB)],
                   halo_send.at[stage, 1], halo_recv.at[stage, 1], right),
        ]

        for d in range(N_BLK):
            for s in range(SHORT):
                if d == 0:
                    fet[s] = fv[wanted[s]]
                else:
                    fet_out[(d - 1) * SHORT + s] = fv[wanted[d * SHORT + s]]
        fet_copies = [
            remote(fet_out.at[pl.ds((d - 1) * SHORT, SHORT)], fet.at[pl.ds((4 - d) * SHORT, SHORT)],
                   fet_send.at[stage, d - 1], fet_recv.at[stage, 3 - d], peers[d])
            for d in (1, 3, 2)
        ]

        def split_own(i, c):
            for u in range(4):
                r = i * 4 + u
                hi, lo = split(fv[r])
                ext[HB + r, :128, :] = hi
                ext[HB + r, 128:, :] = lo
            return c

        lax.fori_loop(0, brows // 4, split_own, 0)

        if stage == 0:
            loads[1].wait()
        terms = []
        for d in range(N_BLK):
            c = lax.rem(b + d, N_BLK)
            for s in range(SHORT):
                terms.append(three(ws[c * SHORT + s].T, ext[HB + srows[c, s]]))
        for s in range(SHORT):
            trm[s] = terms[s]
        for i in range(SHORT, N_BLK * SHORT):
            trm_out[i - SHORT] = terms[i]

        def send_terms(s):
            return [
                remote(trm_out.at[(d - 1) * SHORT + s], trm.at[(4 - d) * SHORT + s],
                       trm_send.at[stage, s, d - 1], trm_recv.at[stage, s, 3 - d], peers[d])
                for d in (1, 3, 2)
            ]

        trm_copies = send_terms(0)
        if stage == 0:
            trm_copies += send_terms(1)

        acc_h[...] = jnp.zeros(acc_h.shape, F32)
        acc_l[...] = jnp.zeros(acc_l.shape, F32)
        acc_y[...] = jnp.zeros(acc_y.shape, F32)

        def halves(i):
            hi = ext[pl.ds(HB + i * per, per), :128, :].reshape(per * 128, 256)
            lo = ext[pl.ds(HB + i * per, per), 128:, :].reshape(per * 128, 256)
            return hi, lo

        def gram(i, c):
            hi, lo = halves(i)
            both = dot_t(hi, jnp.concatenate([hi, lo], axis=1))
            acc_h[...] += both[:, :256] + dot_t(lo, lo)
            acc_l[...] += both[:, 256:]
            return c

        lax.fori_loop(0, brows // per, gram, 0)
        low = acc_l[...]
        x_h[pl.ds(x_at, 256)] = acc_h[...] + (low + low.T)
        if stage == 1:
            reduce1.pair()

        if stage == 0:
            make_plan()
            loads[2].wait()

        def backward(i, carry):
            terms = []
            for u in range(back):
                m = plan[PERM, i * back + u]
                terms.append(three(wn[m].T, ext[HB + lax.div(m, NEAR_PER)]))
            run = seg[i * back]
            for u in range(back):
                run = run * plan[KEEP, i * back + u].astype(F32) + terms[u]
                seg[i * back + u + 1] = run
            return carry

        lax.fori_loop(0, brows * NEAR_PER // back, backward, 0)
        for q in range(HB):
            rim_out[q] = seg[plan[LAST, q]]
            rim_out[HB + q] = seg[plan[LAST, HB + brows + q]]
        rim_copies = [
            remote(rim_out.at[pl.ds(0, HB)], rim_in.at[stage, pl.ds(HB, HB)],
                   rim_send.at[stage, 0], rim_recv.at[stage, 0], left),
            remote(rim_out.at[pl.ds(HB, HB)], rim_in.at[stage, pl.ds(0, HB)],
                   rim_send.at[stage, 1], rim_recv.at[stage, 1], right),
        ]
        if stage == 1:
            reduce1.scatter()

        for copy in halo_copies:
            copy.wait()
        for q in range(2 * HB):
            hi, lo = split(halo[stage, q])
            at = q if q < HB else q + brows
            ext[at, :128, :] = hi
            ext[at, 128:, :] = lo

        def half_diag(r):
            d = dsp[r]
            return jnp.concatenate([d, d], axis=1) * fv[r]

        def forward(i, c):
            sums = []
            for u in range(rows_at_once):
                lhs, rhs = [], []
                for j in range(NEAR_PER):
                    m = (i * rows_at_once + u) * NEAR_PER + j
                    hi, lo = split(wn[m])
                    e = ext[cols[m]]
                    lhs += [hi, hi, lo]
                    rhs += [e, e[:128]]
                sums.append(dot(jnp.concatenate(lhs, axis=1), jnp.concatenate(rhs, axis=0)))
            for u in range(rows_at_once):
                r = i * rows_at_once + u
                out[r] = half_diag(r) + sums[u]
            return c

        lax.fori_loop(0, brows // rows_at_once, forward, 0)
        if stage == 1:
            reduce1.across()
            trm_copies += send_terms(1)

        for copy in fet_copies:
            copy.wait()
        terms = []
        for i in range(N_BLK * SHORT):
            n = plan[SPERM, i]
            slot = lax.rem(lax.div(n, SHORT) + N_BLK - b, N_BLK) * SHORT + lax.rem(n, SHORT)
            hi, lo = split(fet[slot])
            terms.append(three(ws[n], jnp.concatenate([hi, lo], axis=0)))
        run = rseg[0]
        for i in range(N_BLK * SHORT):
            run = run * plan[SKEEP, i].astype(F32) + terms[i]
            rseg[i + 1] = run

        def gram_y(i, c):
            parts = []
            for u in range(per):
                r = i * per + u
                f = out[r] + rseg[plan[SLAST, r]]
                out[r] = f
                parts.append(f)
            fh, fl = split(jnp.concatenate(parts, axis=0))
            hi, lo = halves(i)
            both = dot_t(hi, jnp.concatenate([fh, fl], axis=1))
            acc_y[...] += (both[:, :256] + both[:, 256:]) + dot_t(lo, fh)
            return c

        lax.fori_loop(0, brows // per, gram_y, 0)
        y = acc_y[...]
        x_y[pl.ds(256 if stage == 0 else 0, 256)] = y + y.T
        if stage == 1:
            reduce2.scatter()
            reduce1.gather()

        for copy in trm_copies:
            copy.wait()
        run = tseg[0]
        for i in range(N_BLK * SHORT):
            run = run * tplan[KEEP, i].astype(F32) + trm[tplan[PERM, i]]
            tseg[i + 1] = run

        def finish(i, c):
            for u in range(4):
                r = i * 4 + u
                out[r] = (out[r] + half_diag(r)) + (seg[plan[LAST, HB + r]] + tseg[tplan[LAST, r]])
            return c

        if stage == 1:
            reduce2.across()
        lax.fori_loop(0, brows // 4, finish, 0)
        if stage == 1:
            reduce1.regroup()
        for copy in rim_copies:
            copy.wait()
        for q in range(HB):
            out[q] = out[q] + rim_in[stage, q]
            out[brows - HB + q] = out[brows - HB + q] + rim_in[stage, HB + q]

    operate(0, f0, f1, x1, x1, 0, trm_0, fet_0)
    copy1 = pltpu.make_async_copy(f1, image, out_sem.at[0])
    copy1.start()
    operate(1, f1, f0, x1, x2, 512, trm_1, fet_1)
    copy2 = pltpu.make_async_copy(f0, image2, out_sem.at[1])
    copy2.start()
    reduce2.gather()
    reduce1.finish()
    reduce2.finish()
    copy1.wait()
    copy2.wait()


def krylov(near_cols, short_rows, short_cols, field, diag, near, short):
    brows = field.shape[0]
    smem = pl.BlockSpec(memory_space=pltpu.SMEM)
    vmem = pl.BlockSpec(memory_space=pltpu.VMEM)
    hbm = pl.BlockSpec(memory_space=pl.ANY)
    n_grp = 32
    dma = pltpu.SemaphoreType.DMA

    def block(*n):
        return pltpu.VMEM(n + (128, 256), F32)

    def words(*n):
        return pltpu.VMEM(n + (8, 128), jnp.int32)

    def reduce_scratch(n, piece):
        return [
            pltpu.VMEM((n - 1, piece, 256), F32), pltpu.VMEM((piece, 256), F32),
            pltpu.VMEM((N_BLK - 1, piece, 256), F32), pltpu.VMEM((piece, 256), F32),
        ]

    return pl.pallas_call(
        krylov_kernel,
        out_shape=(
            jax.ShapeDtypeStruct(field.shape, F32),
            jax.ShapeDtypeStruct(field.shape, F32),
            jax.ShapeDtypeStruct((768, 256), F32),
            jax.ShapeDtypeStruct((256, 256), F32),
        ),
        in_specs=[smem, smem, smem, vmem, hbm, vmem, hbm, hbm],
        out_specs=(hbm, hbm, vmem, vmem),
        scratch_shapes=[
            block(brows), block(brows),
            pltpu.VMEM((brows + 2 * HB, 256, 256), BF16),
            pltpu.VMEM(near.shape, F32),
            pltpu.VMEM(short.shape, F32),
            pltpu.VMEM((brows, 128, 128), F32),
            block(brows * NEAR_PER + 1), block(9), block(9),
            block(2, 2 * HB), block(2 * HB), block(2, 2 * HB),
            block(6), block(8), block(8), block(6), block(8), block(8),
            words(), words(3), pltpu.SMEM((3, 8, 128), jnp.int32), words(),
            words(), pltpu.SMEM((8, 128), jnp.int32), words(), pltpu.SMEM((8, 128), jnp.int32),
            pltpu.VMEM((256, 256), F32), pltpu.VMEM((256, 256), F32), pltpu.VMEM((256, 256), F32),
            pltpu.VMEM((768, 256), F32), pltpu.VMEM((384, 256), F32), pltpu.VMEM((384, 256), F32),
            *reduce_scratch(16, 24),
            pltpu.VMEM((256, 256), F32), *reduce_scratch(32, 8),
            dma((3,)), dma((2,)), dma((3,)), dma((3,)), dma((3,)),
            dma((2, 2)), dma((2, 2)), dma((2, 2, 3)), dma((2, 2, 3)), dma((2, 3)), dma((2, 3)),
            dma((2, 2)), dma((2, 2)),
            dma((4,)), dma((4, n_grp // 2 - 1)), dma((2, 3)), dma((4, n_grp - 1)), dma((2, 3)),
        ],
        compiler_params=pltpu.CompilerParams(
            collective_id=0, has_side_effects=True, vmem_limit_bytes=VMEM_LIMIT
        ),
        name="krylov",
    )(near_cols, short_rows, short_cols, near_cols.reshape(1, -1), field, diag, near, short)


def mm(a, b):
    return jnp.dot(a, b, precision=HIGHEST, preferred_element_type=F32)


def mm3(a, b):
    return jnp.dot(a, b, precision=lax.Precision.HIGH, preferred_element_type=F32)


def tail_kernel(
    grams1, grams2, r0, q1, s2, sol, res,
    rv, qv, sv, sol_v, res_v, w_sol, w_res, work, load_sem, sol_sem, res_sem,
):
    loads = [
        pltpu.make_async_copy(src, dst, load_sem.at[i])
        for i, (src, dst) in enumerate(((r0, rv), (q1, qv), (s2, sv)))
    ]
    for copy in loads:
        copy.start()
    n = 256
    diagonal = lax.broadcasted_iota(jnp.int32, (n, n), 0) == lax.broadcasted_iota(jnp.int32, (n, n), 1)
    eye = jnp.where(diagonal, 1.0, 0.0)

    def scales(m):
        kept = jnp.where(diagonal, m, 0.0)
        return lax.rsqrt(jnp.sum(kept, axis=0, keepdims=True)), lax.rsqrt(jnp.sum(kept, axis=1, keepdims=True))

    def size(m):
        return jnp.max(jnp.abs(m))

    def square(limit):
        def step(state):
            e = work[n:, :]
            both = mm3(work[...], e)
            work[:n, :] = work[:n, :] + both[:n]
            work[n:, :] = both[n:]
            return state[0] + 1, size(both[n:])

        return lax.while_loop(
            lambda state: (state[0] < limit) & (state[1] > 1e-5), step, (jnp.int32(0), size(work[n:, :]))
        )[1]

    def polish(m):
        def step(state):
            x = work[:n, :]
            e = eye - mm(m, x)
            work[:n, :] = x + mm(x, e)
            return state[0] + 1, size(e)

        lax.while_loop(lambda state: (state[0] < 6) & (state[1] > 1e-4), step, (jnp.int32(0), F32(1.0)))

    def spd_inverse(m, guess):
        along, down = scales(m)
        scaled = m * along * down

        def from_norm():
            bound = jnp.max(jnp.sum(jnp.abs(scaled), axis=1, keepdims=True))
            work[:n, :] = eye / bound
            work[n:, :] = eye - scaled / bound
            square(48)
            polish(scaled)

        if guess is None:
            from_norm()
        else:
            near = guess / along / down
            z = mm(scaled, near)
            tau = n / jnp.sum(jnp.where(diagonal, z, 0.0))
            work[:n, :] = near * tau
            work[n:, :] = eye - z * tau
            left = square(6)

            @pl.when(jnp.logical_not(left <= 1e-5))
            def _():
                from_norm()

        return work[:n, :] * along * down

    def solve(matrix, inverse, rhs):
        x = mm3(inverse, rhs)
        return x + mm3(inverse, rhs - mm(matrix, x))

    rr0, g01, g11 = (grams1[i * n : (i + 1) * n, :] for i in range(3))
    g12 = grams2[...]
    inv0 = spd_inverse(rr0, None)
    a1 = solve(g01, spd_inverse(g01, inv0), rr0)
    ga = mm(g01, a1)
    g11a = mm(g11, a1)
    rr1 = (rr0 - ga) + (mm(a1.T, g11a) - ga.T)
    rr1 = 0.5 * (rr1 + rr1.T)
    t = eye + solve(rr0, inv0, rr1)
    cross = mm(t.T, g11a)
    pq2 = (mm(t.T, mm(g01, t)) - cross) + (mm(a1.T, mm(g12, a1)) - cross.T)
    pq2 = 0.5 * (pq2 + pq2.T)
    a2 = solve(pq2, spd_inverse(pq2, inv0), rr1)
    c = a1 + mm(t, a2)
    d = mm(a1, a2)
    c_diag = jnp.sum(jnp.where(diagonal, c, 0.0), axis=0, keepdims=True)
    d_diag = jnp.sum(jnp.where(diagonal, d, 0.0), axis=0, keepdims=True)
    c_hi, c_lo = split(jnp.where(diagonal, 0.0, c))
    d_hi, d_lo = split(jnp.where(diagonal, 0.0, d))
    for i, part in enumerate((c_hi, c_lo, c_hi, -d_hi, -d_lo, -d_hi)):
        w_sol[i * n : (i + 1) * n, :] = part
        w_res[i * n : (i + 1) * n, :] = -part

    for copy in loads:
        copy.wait()
    tile = 512
    tiles = rv.shape[0] // tile

    def three(x, y):
        x_hi, x_lo = split(x)
        y_hi, y_lo = split(y)
        return jnp.concatenate([x_hi, x_hi, x_lo, y_hi, y_hi, y_lo], axis=1)

    for i in range(tiles):
        at = pl.ds(i * tile, tile)
        sol_v[at] = (rv[at] * c_diag - qv[at] * d_diag) + dot(three(rv[at], qv[at]), w_sol[...])
        pltpu.make_async_copy(sol_v.at[at], sol.at[at], sol_sem.at[i]).start()
        res_v[at] = (rv[at] - qv[at] * c_diag + sv[at] * d_diag) + dot(three(qv[at], sv[at]), w_res[...])
        pltpu.make_async_copy(res_v.at[at], res.at[at], res_sem.at[i]).start()
    for i in range(tiles):
        at = pl.ds(i * tile, tile)
        pltpu.make_async_copy(sol_v.at[at], sol.at[at], sol_sem.at[i]).wait()
        pltpu.make_async_copy(res_v.at[at], res.at[at], res_sem.at[i]).wait()


def tail(grams1, grams2, r0, q1, s2):
    vmem = pl.BlockSpec(memory_space=pltpu.VMEM)
    hbm = pl.BlockSpec(memory_space=pl.ANY)
    dma = pltpu.SemaphoreType.DMA
    field = pltpu.VMEM(r0.shape, F32)
    return pl.pallas_call(
        tail_kernel,
        out_shape=(jax.ShapeDtypeStruct(r0.shape, F32),) * 2,
        in_specs=[vmem, vmem, hbm, hbm, hbm],
        out_specs=(hbm, hbm),
        scratch_shapes=[
            field, field, field, field, field,
            pltpu.VMEM((1536, 256), BF16), pltpu.VMEM((1536, 256), BF16),
            pltpu.VMEM((512, 256), F32),
            dma((3,)), dma((8,)), dma((8,)),
        ],
        compiler_params=pltpu.CompilerParams(vmem_limit_bytes=VMEM_LIMIT),
        name="tail",
    )(grams1, grams2, r0, q1, s2)


def body(loads, pore_diag, near_blocks, near_cols, short_blocks, short_rows, short_cols):
    rows, cases = loads.shape
    brows = rows // 128
    q1, s2, grams1, grams2 = krylov(
        near_cols, short_rows, short_cols, loads.reshape(brows, 128, cases), pore_diag.reshape(brows, 128),
        near_blocks, short_blocks.reshape(-1, 128, 128),
    )
    return tail(grams1, grams2, loads, q1.reshape(rows, cases), s2.reshape(rows, cases))


def solution(mesh):
    in_specs = (
        P(("blk", "grp"), None),
        P(("blk", "grp")),
        P(("blk", "grp"), None, None),
        P(("blk", "grp")),
        P(("blk", "grp"), None, None, None),
        P(("blk", "grp"), None),
        P(("blk", "grp"), None),
    )
    out_specs = (P(("blk", "grp"), None), P(("blk", "grp"), None))
    return jax.shard_map(body, mesh=mesh, in_specs=in_specs, out_specs=out_specs, check_vma=False)
```

```python
import jax
import jax.numpy as jnp
from jax import lax
from jax.experimental import pallas as pl
from jax.experimental.pallas import tpu as pltpu
from jax.sharding import PartitionSpec as P

NEAR_PER = 3
HB = 4
SHORT = 2
N_BLK = 4
MESH = pl.DeviceIdType.MESH
HIGHEST = lax.Precision.HIGHEST
F32 = jnp.float32
BF16 = jnp.bfloat16
VMEM_LIMIT = 60 * 1024 * 1024

PERM, KEEP, LAST, SPERM, SKEEP, SLAST = range(6)


def split(x):
    hi = x.astype(BF16)
    lo = (x - hi.astype(F32)).astype(BF16)
    return hi, lo


def dot(a, b):
    return jnp.dot(a, b, preferred_element_type=F32)


def dot_t(a, b):
    return lax.dot_general(a, b, (((0,), (0,)), ((), ())), preferred_element_type=F32)


def three(w, e):
    hi, lo = split(w)
    return dot(jnp.concatenate([hi, hi, lo], axis=1), jnp.concatenate([e, e[:128]], axis=0))


def order(keys, n):
    square = (128, 128)
    at_col = lax.broadcasted_iota(jnp.int32, square, 0)
    at_row = lax.broadcasted_iota(jnp.int32, square, 1)
    lane = lax.broadcasted_iota(jnp.int32, (1, 128), 1)
    key = jnp.where(lane < n, keys, 64)
    both = key * 128 + lane
    key_col = jnp.broadcast_to(key, square).T
    both_col = jnp.broadcast_to(both, square).T

    def count(cond):
        return jnp.sum(jnp.where(cond, 1, 0), axis=0, keepdims=True)

    rank = count(both_col < jnp.broadcast_to(both, square))
    hit = jnp.broadcast_to(rank, square).T == at_row
    perm = jnp.sum(jnp.where(hit, at_col, 0), axis=0, keepdims=True)
    placed = jnp.sum(jnp.where(hit, key_col, 0), axis=0, keepdims=True)
    keep = jnp.where(count(key_col < jnp.broadcast_to(placed, square)) < lane, 1, 0)
    begin, end = count(key_col < at_row), count(key_col <= at_row)
    return perm, keep, jnp.where(end > begin, end, 0)


def lanes(values):
    lane = lax.broadcasted_iota(jnp.int32, (1, 128), 1)
    row = jnp.zeros((1, 128), jnp.int32)
    for i, value in enumerate(values):
        row = jnp.where(lane == i, value, row)
    return row


def krylov_kernel(
    cols, srows, scols, cols_row, field, diag, near, short,
    image, image2, grams1, grams2,
    f0, f1, ext, wn, ws, dsp, seg, rseg, tseg, halo, rim_out, rim_in, trm_out, trm_0, trm_1, fet_out, fet_0, fet_1,
    tile, idx_in, idx_sm, keyrow, plan_v, plan, tplan_v, tplan, acc_h, acc_l, acc_y,
    x1, pair1, half1, buf1, part1, zbuf1, mid1, x2, buf2, part2, zbuf2, mid2,
    load_sem, out_sem, idx_sem, idx_send, idx_recv, halo_send, halo_recv, trm_send, trm_recv,
    fet_send, fet_recv, rim_send, rim_recv, pair_sem, red1_sem, zred1_sem, red2_sem, zred2_sem,
):
    brows = f0.shape[0]
    b = lax.axis_index("blk")
    g = lax.axis_index("grp")
    n_grp = lax.axis_size("grp")
    left = (b, lax.rem(g + n_grp - 1, n_grp))
    right = (b, lax.rem(g + 1, n_grp))
    peers = [None] + [(lax.rem(b + d, N_BLK), g) for d in range(1, N_BLK)]

    loads = [
        pltpu.make_async_copy(field, f0, load_sem.at[0]),
        pltpu.make_async_copy(short, ws, load_sem.at[1]),
        pltpu.make_async_copy(near, wn, load_sem.at[2]),
    ]
    for copy in loads:
        copy.start()

    barrier = pltpu.get_barrier_semaphore()

    def greet(i, c):
        peer = (b, lax.rem(g + i, n_grp))
        pl.semaphore_signal(barrier, inc=1, device_id=peer, device_id_type=MESH)
        return c

    lax.fori_loop(1, n_grp, greet, 0)
    for peer in peers[1:]:
        pl.semaphore_signal(barrier, inc=1, device_id=peer, device_id_type=MESH)

    def remote(src, dst, send, recv, peer):
        copy = pltpu.make_async_remote_copy(
            src_ref=src, dst_ref=dst, send_sem=send, recv_sem=recv,
            device_id=peer, device_id_type=MESH,
        )
        copy.start()
        return copy

    sub = lax.broadcasted_iota(jnp.int32, (8, 128), 0)
    lane = lax.broadcasted_iota(jnp.int32, (8, 128), 1)
    own = jnp.zeros((8, 128), jnp.int32)
    for c in range(N_BLK):
        for s in range(SHORT):
            own = jnp.where((sub == c) & (lane == s), scols[s, c], own)
    tile[...] = own
    keyrow[...] = jnp.zeros(keyrow.shape, jnp.int32)
    keyrow[0:1, :96] = cols_row[...]
    plan_v[...] = jnp.zeros(plan_v.shape, jnp.int32)
    plan_v[0:1, :], plan_v[1:2, :], plan_v[2:3, :] = order(keyrow[0:1, :], 96)
    plan_v[3:4, :], plan_v[4:5, :], plan_v[5:6, :] = order(
        lanes([srows[s, c] for c in range(N_BLK) for s in range(SHORT)]), 8
    )
    plan_copy = pltpu.make_async_copy(plan_v, plan, idx_sem.at[0])
    plan_copy.start()

    def spread_diag(r, c):
        dsp[r] = jnp.broadcast_to(diag[pl.ds(r, 1), :], (128, 128)).T * 0.5
        return c

    lax.fori_loop(0, brows, spread_diag, 0)
    seg[0] = jnp.zeros(seg.shape[1:], F32)
    rseg[0] = jnp.zeros(rseg.shape[1:], F32)
    tseg[0] = jnp.zeros(tseg.shape[1:], F32)
    pl.semaphore_wait(barrier, n_grp - 1 + N_BLK - 1)
    idx_copies = [
        remote(tile, idx_in.at[3 - d], idx_send.at[d - 1], idx_recv.at[3 - d], peers[d])
        for d in range(1, N_BLK)
    ]

    def sector_sum(part, zbuf):
        total = jnp.zeros(part.shape, F32)
        for z in range(N_BLK):
            term = jnp.where(b == z, 1.0, 0.0) * part[...]
            for d in range(1, N_BLK):
                term += jnp.where(lax.rem(b + d, N_BLK) == z, 1.0, 0.0) * zbuf[d - 1]
            total += term
        return total

    class Reduce:
        def __init__(self, x, buf, part, zbuf, mid, res, sems, zsems):
            self.x, self.buf, self.part, self.zbuf, self.mid, self.res = x, buf, part, zbuf, mid, res
            self.sems, self.zsems = sems, zsems
            self.rows = x.shape[0] // n_grp

        def piece(self, ref, at):
            return ref.at[pl.ds(pl.multiple_of(at * self.rows, self.rows), self.rows)]

        def each(self, act):
            def step(i, c):
                act(i)
                return c

            lax.fori_loop(1, n_grp, step, 0)

        def spread(self, i):
            t = lax.rem(g + i, n_grp)
            return pltpu.make_async_remote_copy(
                src_ref=self.piece(self.x, t), dst_ref=self.buf.at[n_grp - 1 - i],
                send_sem=self.sems.at[0, i - 1], recv_sem=self.sems.at[1, n_grp - 1 - i],
                device_id=(b, t), device_id_type=MESH,
            )

        def share(self, i):
            t = lax.rem(g + i, n_grp)
            return pltpu.make_async_remote_copy(
                src_ref=self.mid, dst_ref=self.piece(self.res, g),
                send_sem=self.sems.at[2, i - 1], recv_sem=self.sems.at[3, n_grp - 1 - i],
                device_id=(b, t), device_id_type=MESH,
            )

        def scatter(self):
            self.each(lambda i: self.spread(i).start())

        def across(self):
            self.each(lambda i: self.spread(i).wait())
            total = self.x[pl.ds(pl.multiple_of(g * self.rows, self.rows), self.rows)]
            for i in range(n_grp - 1):
                total += self.buf[i]
            self.part[...] = total
            self.copies = [
                remote(self.part, self.zbuf.at[3 - d], self.zsems.at[0, d - 1], self.zsems.at[1, 3 - d], peers[d])
                for d in range(1, N_BLK)
            ]

        def gather(self):
            for copy in self.copies:
                copy.wait()
            total = sector_sum(self.part, self.zbuf)
            self.mid[...] = total
            self.res[pl.ds(pl.multiple_of(g * self.rows, self.rows), self.rows)] = total
            self.each(lambda i: self.share(i).start())

        def finish(self):
            self.each(lambda i: self.share(i).wait())

    class PairReduce:
        def __init__(self, x, pair, half, buf, part, zbuf, mid, res, psems, sems, zsems):
            self.x, self.pair_in, self.half, self.buf = x, pair, half, buf
            self.part, self.zbuf, self.mid, self.res = part, zbuf, mid, res
            self.psems, self.sems, self.zsems = psems, sems, zsems
            self.core, self.plane, self.planes = lax.rem(g, 2), lax.div(g, 2), n_grp // 2
            self.other = (b, self.plane * 2 + 1 - self.core)
            self.half_rows = x.shape[0] // 2
            self.rows = self.half_rows // self.planes

        def halved(self, ref, core):
            return ref.at[pl.ds(pl.multiple_of(core * self.half_rows, self.half_rows), self.half_rows)]

        def each(self, act):
            def step(i, c):
                act(i)
                return c

            lax.fori_loop(1, self.planes, step, 0)

        def spread(self, i):
            t = lax.rem(self.plane + i, self.planes)
            return pltpu.make_async_remote_copy(
                src_ref=self.half.at[pl.ds(pl.multiple_of(t * self.rows, self.rows), self.rows)],
                dst_ref=self.buf.at[self.planes - 1 - i],
                send_sem=self.sems.at[0, i - 1], recv_sem=self.sems.at[1, self.planes - 1 - i],
                device_id=(b, t * 2 + self.core), device_id_type=MESH,
            )

        def own_piece(self):
            at = self.core * self.half_rows + self.plane * self.rows
            return pl.ds(pl.multiple_of(at, self.rows), self.rows)

        def share(self, i):
            t = lax.rem(self.plane + i, self.planes)
            return pltpu.make_async_remote_copy(
                src_ref=self.mid, dst_ref=self.res.at[self.own_piece()],
                send_sem=self.sems.at[2, i - 1], recv_sem=self.sems.at[3, self.planes - 1 - i],
                device_id=(b, t * 2 + self.core), device_id_type=MESH,
            )

        def pair(self):
            self.paired = remote(
                self.halved(self.x, 1 - self.core), self.pair_in, self.psems.at[0], self.psems.at[1], self.other
            )

        def scatter(self):
            self.paired.wait()
            at = pl.multiple_of(self.core * self.half_rows, self.half_rows)
            self.half[...] = self.x[pl.ds(at, self.half_rows)] + self.pair_in[...]
            self.each(lambda i: self.spread(i).start())

        def across(self):
            self.each(lambda i: self.spread(i).wait())
            total = self.half[pl.ds(pl.multiple_of(self.plane * self.rows, self.rows), self.rows)]
            for i in range(self.planes - 1):
                total += self.buf[i]
            self.part[...] = total
            self.copies = [
                remote(self.part, self.zbuf.at[3 - d], self.zsems.at[0, d - 1], self.zsems.at[1, 3 - d], peers[d])
                for d in range(1, N_BLK)
            ]

        def gather(self):
            for copy in self.copies:
                copy.wait()
            total = sector_sum(self.part, self.zbuf)
            self.mid[...] = total
            self.res[self.own_piece()] = total
            self.each(lambda i: self.share(i).start())

        def regroup(self):
            self.each(lambda i: self.share(i).wait())
            mine = self.halved(self.res, self.core)
            self.paired = remote(mine, mine, self.psems.at[2], self.psems.at[3], self.other)

        def finish(self):
            self.paired.wait()

    reduce1 = PairReduce(x1, pair1, half1, buf1, part1, zbuf1, mid1, grams1, pair_sem, red1_sem, zred1_sem)
    reduce2 = Reduce(x2, buf2, part2, zbuf2, mid2, grams2, red2_sem, zred2_sem)

    per = 8
    back = 12
    rows_at_once = 8

    def learn_wanted():
        for copy in idx_copies:
            copy.wait()
        idx_copy = pltpu.make_async_copy(idx_in, idx_sm, idx_sem.at[1])
        idx_copy.start()
        idx_copy.wait()
        wanted = [scols[s, b] for s in range(SHORT)]
        for d in range(1, N_BLK):
            wanted += [idx_sm[d - 1, b, s] for s in range(SHORT)]
        tplan_v[...] = jnp.zeros(tplan_v.shape, jnp.int32)
        tplan_v[0:1, :], tplan_v[1:2, :], tplan_v[2:3, :] = order(lanes(wanted), 8)
        tplan_copy = pltpu.make_async_copy(tplan_v, tplan, idx_sem.at[2])
        tplan_copy.start()
        return wanted, tplan_copy

    known = []

    def operate(stage, fv, out, x_h, x_y, x_at, trm, fet):
        if stage == 0:
            loads[0].wait()
        halo_copies = [
            remote(fv.at[pl.ds(0, HB)], halo.at[stage, pl.ds(HB, HB)],
                   halo_send.at[stage, 0], halo_recv.at[stage, 0], left),
            remote(fv.at[pl.ds(brows - HB, HB)], halo.at[stage, pl.ds(0, HB)],
                   halo_send.at[stage, 1], halo_recv.at[stage, 1], right),
        ]

        def send_fetch(wanted):
            for d in range(N_BLK):
                for s in range(SHORT):
                    if d == 0:
                        fet[s] = fv[wanted[s]]
                    else:
                        fet_out[(d - 1) * SHORT + s] = fv[wanted[d * SHORT + s]]
            return [
                remote(fet_out.at[pl.ds((d - 1) * SHORT, SHORT)], fet.at[pl.ds((4 - d) * SHORT, SHORT)],
                       fet_send.at[stage, d - 1], fet_recv.at[stage, 3 - d], peers[d])
                for d in (1, 3, 2)
            ]

        if stage == 1:
            fet_copies = send_fetch(known[0])

        if stage == 0:
            loads[1].wait()
        terms = []
        for d in range(N_BLK):
            c = lax.rem(b + d, N_BLK)
            for s in range(SHORT):
                terms.append(three(ws[c * SHORT + s].T, jnp.concatenate(split(fv[srows[s, c]]), axis=0)))
        for s in range(SHORT):
            trm[s] = terms[s]
        for i in range(SHORT, N_BLK * SHORT):
            trm_out[i - SHORT] = terms[i]

        def send_terms(s):
            return [
                remote(trm_out.at[(d - 1) * SHORT + s], trm.at[(4 - d) * SHORT + s],
                       trm_send.at[stage, s, d - 1], trm_recv.at[stage, s, 3 - d], peers[d])
                for d in (1, 3, 2)
            ]

        trm_copies = send_terms(0)
        trm_copies += send_terms(1)
        if stage == 0:
            known.extend(learn_wanted())
            fet_copies = send_fetch(known[0])

        def split_own(i, c):
            for u in range(4):
                r = i * 4 + u
                hi, lo = split(fv[r])
                ext[HB + r, :128, :] = hi
                ext[HB + r, 128:, :] = lo
            return c

        lax.fori_loop(0, brows // 4, split_own, 0)

        acc_h[...] = jnp.zeros(acc_h.shape, F32)
        acc_l[...] = jnp.zeros(acc_l.shape, F32)
        acc_y[...] = jnp.zeros(acc_y.shape, F32)

        def halves(i):
            hi = ext[pl.ds(HB + i * per, per), :128, :].reshape(per * 128, 256)
            lo = ext[pl.ds(HB + i * per, per), 128:, :].reshape(per * 128, 256)
            return hi, lo

        def gram(i, c):
            hi, lo = halves(i)
            both = dot_t(hi, jnp.concatenate([hi, lo], axis=1))
            acc_h[...] += both[:, :256] + dot_t(lo, lo)
            acc_l[...] += both[:, 256:]
            return c

        lax.fori_loop(0, brows // per, gram, 0)
        low = acc_l[...]
        x_h[pl.ds(x_at, 256)] = acc_h[...] + (low + low.T)
        if stage == 1:
            reduce1.pair()

        if stage == 0:
            plan_copy.wait()
            known[1].wait()
            loads[2].wait()

        def backward(i, carry):
            terms = []
            for u in range(back):
                m = plan[PERM, i * back + u]
                terms.append(three(wn[m].T, ext[HB + lax.div(m, NEAR_PER)]))
            run = seg[i * back]
            for u in range(back):
                run = run * plan[KEEP, i * back + u].astype(F32) + terms[u]
                seg[i * back + u + 1] = run
            return carry

        lax.fori_loop(0, brows * NEAR_PER // back, backward, 0)
        for q in range(HB):
            rim_out[q] = seg[plan[LAST, q]]
            rim_out[HB + q] = seg[plan[LAST, HB + brows + q]]
        rim_copies = [
            remote(rim_out.at[pl.ds(0, HB)], rim_in.at[stage, pl.ds(HB, HB)],
                   rim_send.at[stage, 0], rim_recv.at[stage, 0], left),
            remote(rim_out.at[pl.ds(HB, HB)], rim_in.at[stage, pl.ds(0, HB)],
                   rim_send.at[stage, 1], rim_recv.at[stage, 1], right),
        ]
        if stage == 1:
            reduce1.scatter()

        for copy in halo_copies:
            copy.wait()
        for q in range(2 * HB):
            hi, lo = split(halo[stage, q])
            at = q if q < HB else q + brows
            ext[at, :128, :] = hi
            ext[at, 128:, :] = lo

        def half_diag(r):
            d = dsp[r]
            return jnp.concatenate([d, d], axis=1) * fv[r]

        def forward(i, c):
            sums = []
            for u in range(rows_at_once):
                lhs, rhs = [], []
                for j in range(NEAR_PER):
                    m = (i * rows_at_once + u) * NEAR_PER + j
                    hi, lo = split(wn[m])
                    e = ext[cols[m]]
                    lhs += [hi, hi, lo]
                    rhs += [e, e[:128]]
                sums.append(dot(jnp.concatenate(lhs, axis=1), jnp.concatenate(rhs, axis=0)))
            for u in range(rows_at_once):
                r = i * rows_at_once + u
                out[r] = half_diag(r) + sums[u]
            return c

        lax.fori_loop(0, brows // rows_at_once, forward, 0)
        for copy in fet_copies:
            copy.wait()
        terms = []
        for i in range(N_BLK * SHORT):
            n = plan[SPERM, i]
            slot = lax.rem(lax.div(n, SHORT) + N_BLK - b, N_BLK) * SHORT + lax.rem(n, SHORT)
            hi, lo = split(fet[slot])
            terms.append(three(ws[n], jnp.concatenate([hi, lo], axis=0)))
        run = rseg[0]
        for i in range(N_BLK * SHORT):
            run = run * plan[SKEEP, i].astype(F32) + terms[i]
            rseg[i + 1] = run

        def gram_y(i, c):
            parts = []
            for u in range(per):
                r = i * per + u
                f = out[r] + rseg[plan[SLAST, r]]
                out[r] = f
                parts.append(f)
            fh, fl = split(jnp.concatenate(parts, axis=0))
            hi, lo = halves(i)
            both = dot_t(hi, jnp.concatenate([fh, fl], axis=1))
            acc_y[...] += (both[:, :256] + both[:, 256:]) + dot_t(lo, fh)
            return c

        lax.fori_loop(0, brows // per, gram_y, 0)
        y = acc_y[...]
        x_y[pl.ds(256 if stage == 0 else 0, 256)] = y + y.T
        if stage == 1:
            reduce2.scatter()
            reduce1.across()

        for copy in trm_copies:
            copy.wait()
        run = tseg[0]
        for i in range(N_BLK * SHORT):
            run = run * tplan[KEEP, i].astype(F32) + trm[tplan[PERM, i]]
            tseg[i + 1] = run

        def finish(i, c):
            for u in range(4):
                r = i * 4 + u
                out[r] = (out[r] + half_diag(r)) + (seg[plan[LAST, HB + r]] + tseg[tplan[LAST, r]])
            return c

        if stage == 1:
            reduce2.across()
            reduce1.gather()
        lax.fori_loop(0, brows // 4, finish, 0)
        for copy in rim_copies:
            copy.wait()
        for q in range(HB):
            out[q] = out[q] + rim_in[stage, q]
            out[brows - HB + q] = out[brows - HB + q] + rim_in[stage, HB + q]

    operate(0, f0, f1, x1, x1, 0, trm_0, fet_0)
    copy1 = pltpu.make_async_copy(f1, image, out_sem.at[0])
    copy1.start()
    operate(1, f1, f0, x1, x2, 512, trm_1, fet_1)
    copy2 = pltpu.make_async_copy(f0, image2, out_sem.at[1])
    copy2.start()
    reduce2.gather()
    reduce1.regroup()
    reduce1.finish()
    reduce2.finish()
    copy1.wait()
    copy2.wait()


def krylov(near_cols, short_rows, short_cols, field, diag, near, short):
    brows = field.shape[0]
    smem = pl.BlockSpec(memory_space=pltpu.SMEM)
    vmem = pl.BlockSpec(memory_space=pltpu.VMEM)
    hbm = pl.BlockSpec(memory_space=pl.ANY)
    n_grp = 32
    dma = pltpu.SemaphoreType.DMA

    def block(*n):
        return pltpu.VMEM(n + (128, 256), F32)

    def words(*n):
        return pltpu.VMEM(n + (8, 128), jnp.int32)

    def reduce_scratch(n, piece):
        return [
            pltpu.VMEM((n - 1, piece, 256), F32), pltpu.VMEM((piece, 256), F32),
            pltpu.VMEM((N_BLK - 1, piece, 256), F32), pltpu.VMEM((piece, 256), F32),
        ]

    return pl.pallas_call(
        krylov_kernel,
        out_shape=(
            jax.ShapeDtypeStruct(field.shape, F32),
            jax.ShapeDtypeStruct(field.shape, F32),
            jax.ShapeDtypeStruct((768, 256), F32),
            jax.ShapeDtypeStruct((256, 256), F32),
        ),
        in_specs=[smem, smem, smem, vmem, hbm, vmem, hbm, hbm],
        out_specs=(hbm, hbm, vmem, vmem),
        scratch_shapes=[
            block(brows), block(brows),
            pltpu.VMEM((brows + 2 * HB, 256, 256), BF16),
            pltpu.VMEM(near.shape, F32),
            pltpu.VMEM(short.shape, F32),
            pltpu.VMEM((brows, 128, 128), F32),
            block(brows * NEAR_PER + 1), block(9), block(9),
            block(2, 2 * HB), block(2 * HB), block(2, 2 * HB),
            block(6), block(8), block(8), block(6), block(8), block(8),
            words(), words(3), pltpu.SMEM((3, 8, 128), jnp.int32), words(),
            words(), pltpu.SMEM((8, 128), jnp.int32), words(), pltpu.SMEM((8, 128), jnp.int32),
            pltpu.VMEM((256, 256), F32), pltpu.VMEM((256, 256), F32), pltpu.VMEM((256, 256), F32),
            pltpu.VMEM((768, 256), F32), pltpu.VMEM((384, 256), F32), pltpu.VMEM((384, 256), F32),
            *reduce_scratch(16, 24),
            pltpu.VMEM((256, 256), F32), *reduce_scratch(32, 8),
            dma((3,)), dma((2,)), dma((3,)), dma((3,)), dma((3,)),
            dma((2, 2)), dma((2, 2)), dma((2, 2, 3)), dma((2, 2, 3)), dma((2, 3)), dma((2, 3)),
            dma((2, 2)), dma((2, 2)),
            dma((4,)), dma((4, n_grp // 2 - 1)), dma((2, 3)), dma((4, n_grp - 1)), dma((2, 3)),
        ],
        compiler_params=pltpu.CompilerParams(
            collective_id=0, has_side_effects=True, vmem_limit_bytes=VMEM_LIMIT
        ),
        name="krylov",
    )(near_cols, short_rows.T, short_cols.T, near_cols.reshape(1, -1), field, diag, near, short)


def mm(a, b):
    return jnp.dot(a, b, precision=HIGHEST, preferred_element_type=F32)


def mm3(a, b):
    return jnp.dot(a, b, precision=lax.Precision.HIGH, preferred_element_type=F32)


def tail_kernel(
    grams1, grams2, r0, q1, s2, sol, res,
    rv, qv, sv, sol_v, res_v, w_sol, w_res, work, load_sem, sol_sem, res_sem,
):
    loads = [
        pltpu.make_async_copy(src, dst, load_sem.at[i])
        for i, (src, dst) in enumerate(((r0, rv), (q1, qv), (s2, sv)))
    ]
    for copy in loads:
        copy.start()
    n = 256
    diagonal = lax.broadcasted_iota(jnp.int32, (n, n), 0) == lax.broadcasted_iota(jnp.int32, (n, n), 1)
    eye = jnp.where(diagonal, 1.0, 0.0)

    def scales(m):
        kept = jnp.where(diagonal, m, 0.0)
        return lax.rsqrt(jnp.sum(kept, axis=0, keepdims=True)), lax.rsqrt(jnp.sum(kept, axis=1, keepdims=True))

    def size(m):
        return jnp.max(jnp.abs(m))

    def square(limit):
        def step(state):
            e = work[n:, :]
            both = mm3(work[...], e)
            work[:n, :] = work[:n, :] + both[:n]
            work[n:, :] = both[n:]
            return state[0] + 1, size(both[n:])

        return lax.while_loop(
            lambda state: (state[0] < limit) & (state[1] > 1e-5), step, (jnp.int32(0), size(work[n:, :]))
        )[1]

    def polish(m):
        def step(state):
            x = work[:n, :]
            e = eye - mm(m, x)
            work[:n, :] = x + mm(x, e)
            return state[0] + 1, size(e)

        lax.while_loop(lambda state: (state[0] < 6) & (state[1] > 1e-4), step, (jnp.int32(0), F32(1.0)))

    def spd_inverse(m, guess):
        along, down = scales(m)
        scaled = m * along * down

        def from_norm():
            bound = jnp.max(jnp.sum(jnp.abs(scaled), axis=1, keepdims=True))
            work[:n, :] = eye / bound
            work[n:, :] = eye - scaled / bound
            square(48)
            polish(scaled)

        if guess is None:
            from_norm()
        else:
            near = guess / along / down
            z = mm(scaled, near)
            tau = n / jnp.sum(jnp.where(diagonal, z, 0.0))
            work[:n, :] = near * tau
            work[n:, :] = eye - z * tau
            left = square(6)

            @pl.when(jnp.logical_not(left <= 1e-5))
            def _():
                from_norm()

        return work[:n, :] * along * down

    def solve(matrix, inverse, rhs):
        x = mm3(inverse, rhs)
        return x + mm3(inverse, rhs - mm(matrix, x))

    rr0, g01, g11 = (grams1[i * n : (i + 1) * n, :] for i in range(3))
    g12 = grams2[...]
    inv0 = spd_inverse(rr0, None)
    a1 = solve(g01, spd_inverse(g01, inv0), rr0)
    ga = mm(g01, a1)
    g11a = mm(g11, a1)
    rr1 = (rr0 - ga) + (mm(a1.T, g11a) - ga.T)
    rr1 = 0.5 * (rr1 + rr1.T)
    t = eye + solve(rr0, inv0, rr1)
    cross = mm(t.T, g11a)
    pq2 = (mm(t.T, mm(g01, t)) - cross) + (mm(a1.T, mm(g12, a1)) - cross.T)
    pq2 = 0.5 * (pq2 + pq2.T)
    a2 = solve(pq2, spd_inverse(pq2, inv0), rr1)
    c = a1 + mm(t, a2)
    d = mm(a1, a2)
    c_diag = jnp.sum(jnp.where(diagonal, c, 0.0), axis=0, keepdims=True)
    d_diag = jnp.sum(jnp.where(diagonal, d, 0.0), axis=0, keepdims=True)
    c_hi, c_lo = split(jnp.where(diagonal, 0.0, c))
    d_hi, d_lo = split(jnp.where(diagonal, 0.0, d))
    for i, part in enumerate((c_hi, c_lo, c_hi, -d_hi, -d_lo, -d_hi)):
        w_sol[i * n : (i + 1) * n, :] = part
        w_res[i * n : (i + 1) * n, :] = -part

    for copy in loads:
        copy.wait()
    tile = 512
    tiles = rv.shape[0] // tile

    def three(x, y):
        x_hi, x_lo = split(x)
        y_hi, y_lo = split(y)
        return jnp.concatenate([x_hi, x_hi, x_lo, y_hi, y_hi, y_lo], axis=1)

    for i in range(tiles):
        at = pl.ds(i * tile, tile)
        sol_v[at] = (rv[at] * c_diag - qv[at] * d_diag) + dot(three(rv[at], qv[at]), w_sol[...])
        pltpu.make_async_copy(sol_v.at[at], sol.at[at], sol_sem.at[i]).start()
        res_v[at] = (rv[at] - qv[at] * c_diag + sv[at] * d_diag) + dot(three(qv[at], sv[at]), w_res[...])
        pltpu.make_async_copy(res_v.at[at], res.at[at], res_sem.at[i]).start()
    for i in range(tiles):
        at = pl.ds(i * tile, tile)
        pltpu.make_async_copy(sol_v.at[at], sol.at[at], sol_sem.at[i]).wait()
        pltpu.make_async_copy(res_v.at[at], res.at[at], res_sem.at[i]).wait()


def tail(grams1, grams2, r0, q1, s2):
    vmem = pl.BlockSpec(memory_space=pltpu.VMEM)
    hbm = pl.BlockSpec(memory_space=pl.ANY)
    dma = pltpu.SemaphoreType.DMA
    field = pltpu.VMEM(r0.shape, F32)
    return pl.pallas_call(
        tail_kernel,
        out_shape=(jax.ShapeDtypeStruct(r0.shape, F32),) * 2,
        in_specs=[vmem, vmem, hbm, hbm, hbm],
        out_specs=(hbm, hbm),
        scratch_shapes=[
            field, field, field, field, field,
            pltpu.VMEM((1536, 256), BF16), pltpu.VMEM((1536, 256), BF16),
            pltpu.VMEM((512, 256), F32),
            dma((3,)), dma((8,)), dma((8,)),
        ],
        compiler_params=pltpu.CompilerParams(vmem_limit_bytes=VMEM_LIMIT),
        name="tail",
    )(grams1, grams2, r0, q1, s2)


def body(loads, pore_diag, near_blocks, near_cols, short_blocks, short_rows, short_cols):
    rows, cases = loads.shape
    brows = rows // 128
    q1, s2, grams1, grams2 = krylov(
        near_cols, short_rows, short_cols, loads.reshape(brows, 128, cases), pore_diag.reshape(brows, 128),
        near_blocks, short_blocks.reshape(-1, 128, 128),
    )
    return tail(grams1, grams2, loads, q1.reshape(rows, cases), s2.reshape(rows, cases))


def solution(mesh):
    in_specs = (
        P(("blk", "grp"), None),
        P(("blk", "grp")),
        P(("blk", "grp"), None, None),
        P(("blk", "grp")),
        P(("blk", "grp"), None, None, None),
        P(("blk", "grp"), None),
        P(("blk", "grp"), None),
    )
    out_specs = (P(("blk", "grp"), None), P(("blk", "grp"), None))
    return jax.shard_map(body, mesh=mesh, in_specs=in_specs, out_specs=out_specs, check_vma=False)
```

```python
import jax
import jax.numpy as jnp
from jax import lax
from jax.experimental import pallas as pl
from jax.experimental.pallas import tpu as pltpu
from jax.sharding import PartitionSpec as P

NEAR_PER = 3
HB = 4
SHORT = 2
N_BLK = 4
MESH = pl.DeviceIdType.MESH
HIGHEST = lax.Precision.HIGHEST
F32 = jnp.float32
BF16 = jnp.bfloat16
VMEM_LIMIT = 60 * 1024 * 1024

PERM, KEEP, LAST, SPERM, SKEEP, SLAST = range(6)


def split(x):
    hi = x.astype(BF16)
    lo = (x - hi.astype(F32)).astype(BF16)
    return hi, lo


def dot(a, b):
    return jnp.dot(a, b, preferred_element_type=F32)


def dot_t(a, b):
    return lax.dot_general(a, b, (((0,), (0,)), ((), ())), preferred_element_type=F32)


def mm(a, b):
    return jnp.dot(a, b, precision=HIGHEST, preferred_element_type=F32)


def mm3(a, b):
    return jnp.dot(a, b, precision=lax.Precision.HIGH, preferred_element_type=F32)


def on_diagonal():
    at = (256, 256)
    return lax.broadcasted_iota(jnp.int32, at, 0) == lax.broadcasted_iota(jnp.int32, at, 1)


def identity():
    return jnp.where(on_diagonal(), 1.0, 0.0)


def scales(m):
    kept = jnp.where(on_diagonal(), m, 0.0)
    return lax.rsqrt(jnp.sum(kept, axis=0, keepdims=True)), lax.rsqrt(jnp.sum(kept, axis=1, keepdims=True))


def three(w, e):
    hi, lo = split(w)
    return dot(jnp.concatenate([hi, hi, lo], axis=1), jnp.concatenate([e, e[:128]], axis=0))


def order(keys, n):
    square = (128, 128)
    at_col = lax.broadcasted_iota(jnp.int32, square, 0)
    at_row = lax.broadcasted_iota(jnp.int32, square, 1)
    lane = lax.broadcasted_iota(jnp.int32, (1, 128), 1)
    key = jnp.where(lane < n, keys, 64)
    both = key * 128 + lane
    key_col = jnp.broadcast_to(key, square).T
    both_col = jnp.broadcast_to(both, square).T

    def count(cond):
        return jnp.sum(jnp.where(cond, 1, 0), axis=0, keepdims=True)

    rank = count(both_col < jnp.broadcast_to(both, square))
    hit = jnp.broadcast_to(rank, square).T == at_row
    perm = jnp.sum(jnp.where(hit, at_col, 0), axis=0, keepdims=True)
    placed = jnp.sum(jnp.where(hit, key_col, 0), axis=0, keepdims=True)
    keep = jnp.where(count(key_col < jnp.broadcast_to(placed, square)) < lane, 1, 0)
    begin, end = count(key_col < at_row), count(key_col <= at_row)
    return perm, keep, jnp.where(end > begin, end, 0)


def lanes(values):
    lane = lax.broadcasted_iota(jnp.int32, (1, 128), 1)
    row = jnp.zeros((1, 128), jnp.int32)
    for i, value in enumerate(values):
        row = jnp.where(lane == i, value, row)
    return row


def krylov_kernel(
    cols, srows, scols, cols_row, field, diag, near, short,
    image, image2, grams1, grams3, grams2, inverse0,
    f0, f1, ext, wn, ws, dsp, seg, rseg, tseg, halo, rim_out, rim_in, trm_out, trm_0, trm_1, fet_out, fet_0, fet_1,
    tile, idx_in, idx_sm, keyrow, plan_v, plan, tplan_v, tplan, acc_h, acc_l, acc_y,
    x1, buf1, part1, zbuf1, mid1, x2, buf2, part2, zbuf2, mid2,
    x3, buf3, part3, zbuf3, mid3, work, along, down,
    load_sem, out_sem, idx_sem, idx_send, idx_recv, halo_send, halo_recv, trm_send, trm_recv,
    fet_send, fet_recv, rim_send, rim_recv, red1_sem, zred1_sem, red2_sem, zred2_sem, red3_sem, zred3_sem,
):
    brows = f0.shape[0]
    b = lax.axis_index("blk")
    g = lax.axis_index("grp")
    n_grp = lax.axis_size("grp")
    left = (b, lax.rem(g + n_grp - 1, n_grp))
    right = (b, lax.rem(g + 1, n_grp))
    peers = [None] + [(lax.rem(b + d, N_BLK), g) for d in range(1, N_BLK)]

    loads = [
        pltpu.make_async_copy(field, f0, load_sem.at[0]),
        pltpu.make_async_copy(short, ws, load_sem.at[1]),
        pltpu.make_async_copy(near, wn, load_sem.at[2]),
    ]
    for copy in loads:
        copy.start()

    barrier = pltpu.get_barrier_semaphore()

    def greet(i, c):
        peer = (b, lax.rem(g + i, n_grp))
        pl.semaphore_signal(barrier, inc=1, device_id=peer, device_id_type=MESH)
        return c

    lax.fori_loop(1, n_grp, greet, 0)
    for peer in peers[1:]:
        pl.semaphore_signal(barrier, inc=1, device_id=peer, device_id_type=MESH)

    def remote(src, dst, send, recv, peer):
        copy = pltpu.make_async_remote_copy(
            src_ref=src, dst_ref=dst, send_sem=send, recv_sem=recv,
            device_id=peer, device_id_type=MESH,
        )
        copy.start()
        return copy

    sub = lax.broadcasted_iota(jnp.int32, (8, 128), 0)
    lane = lax.broadcasted_iota(jnp.int32, (8, 128), 1)
    own = jnp.zeros((8, 128), jnp.int32)
    for c in range(N_BLK):
        for s in range(SHORT):
            own = jnp.where((sub == c) & (lane == s), scols[s, c], own)
    tile[...] = own
    keyrow[...] = jnp.zeros(keyrow.shape, jnp.int32)
    keyrow[0:1, :96] = cols_row[...]
    plan_v[...] = jnp.zeros(plan_v.shape, jnp.int32)
    plan_v[0:1, :], plan_v[1:2, :], plan_v[2:3, :] = order(keyrow[0:1, :], 96)
    plan_v[3:4, :], plan_v[4:5, :], plan_v[5:6, :] = order(
        lanes([srows[s, c] for c in range(N_BLK) for s in range(SHORT)]), 8
    )
    plan_copy = pltpu.make_async_copy(plan_v, plan, idx_sem.at[0])
    plan_copy.start()

    seg[0] = jnp.zeros(seg.shape[1:], F32)
    rseg[0] = jnp.zeros(rseg.shape[1:], F32)
    tseg[0] = jnp.zeros(tseg.shape[1:], F32)
    pl.semaphore_wait(barrier, n_grp - 1 + N_BLK - 1)
    idx_copies = [
        remote(tile, idx_in.at[3 - d], idx_send.at[d - 1], idx_recv.at[3 - d], peers[d])
        for d in range(1, N_BLK)
    ]

    def sector_sum(part, zbuf):
        total = jnp.zeros(part.shape, F32)
        for z in range(N_BLK):
            term = jnp.where(b == z, 1.0, 0.0) * part[...]
            for d in range(1, N_BLK):
                term += jnp.where(lax.rem(b + d, N_BLK) == z, 1.0, 0.0) * zbuf[d - 1]
            total += term
        return total

    class Reduce:
        def __init__(self, x, buf, part, zbuf, mid, res, sems, zsems):
            self.x, self.buf, self.part, self.zbuf, self.mid, self.res = x, buf, part, zbuf, mid, res
            self.sems, self.zsems = sems, zsems
            self.rows = x.shape[0] // n_grp

        def piece(self, ref, at):
            return ref.at[pl.ds(pl.multiple_of(at * self.rows, self.rows), self.rows)]

        def each(self, act):
            def step(i, c):
                act(i)
                return c

            lax.fori_loop(1, n_grp, step, 0)

        def spread(self, i):
            t = lax.rem(g + i, n_grp)
            return pltpu.make_async_remote_copy(
                src_ref=self.piece(self.x, t), dst_ref=self.buf.at[n_grp - 1 - i],
                send_sem=self.sems.at[0, i - 1], recv_sem=self.sems.at[1, n_grp - 1 - i],
                device_id=(b, t), device_id_type=MESH,
            )

        def share(self, i):
            t = lax.rem(g + i, n_grp)
            return pltpu.make_async_remote_copy(
                src_ref=self.mid, dst_ref=self.piece(self.res, g),
                send_sem=self.sems.at[2, i - 1], recv_sem=self.sems.at[3, n_grp - 1 - i],
                device_id=(b, t), device_id_type=MESH,
            )

        def scatter(self):
            self.each(lambda i: self.spread(i).start())

        def across(self):
            self.each(lambda i: self.spread(i).wait())
            total = self.x[pl.ds(pl.multiple_of(g * self.rows, self.rows), self.rows)]
            for i in range(n_grp - 1):
                total += self.buf[i]
            self.part[...] = total
            self.copies = [
                remote(self.part, self.zbuf.at[3 - d], self.zsems.at[0, d - 1], self.zsems.at[1, 3 - d], peers[d])
                for d in range(1, N_BLK)
            ]

        def gather(self):
            for copy in self.copies:
                copy.wait()
            total = sector_sum(self.part, self.zbuf)
            self.mid[...] = total
            self.res[pl.ds(pl.multiple_of(g * self.rows, self.rows), self.rows)] = total
            self.each(lambda i: self.share(i).start())

        def finish(self):
            self.each(lambda i: self.share(i).wait())

    reduce1 = Reduce(x1, buf1, part1, zbuf1, mid1, grams1, red1_sem, zred1_sem)
    reduce3 = Reduce(x3, buf3, part3, zbuf3, mid3, grams3, red3_sem, zred3_sem)
    reduce2 = Reduce(x2, buf2, part2, zbuf2, mid2, grams2, red2_sem, zred2_sem)

    def start_inverse():
        rr0 = grams1[pl.ds(0, 256)]
        along[...], down[...] = scales(rr0)
        scaled = rr0 * along[...] * down[...]
        bound = jnp.max(jnp.sum(jnp.abs(scaled), axis=1, keepdims=True))
        work[:256] = identity() / bound
        work[256:] = identity() - scaled / bound

    def double_inverse(times):
        def step(i, c):
            both = mm3(work[...], work[256:])
            work[:256] = work[:256] + both[:256]
            work[256:] = both[256:]
            return c

        lax.fori_loop(0, times, step, 0)

    per = 8
    back = 12
    rows_at_once = 8

    def learn_wanted():
        for copy in idx_copies:
            copy.wait()
        idx_copy = pltpu.make_async_copy(idx_in, idx_sm, idx_sem.at[1])
        idx_copy.start()
        idx_copy.wait()
        wanted = [scols[s, b] for s in range(SHORT)]
        for d in range(1, N_BLK):
            wanted += [idx_sm[d - 1, b, s] for s in range(SHORT)]
        return wanted

    def order_wanted(wanted):
        tplan_v[...] = jnp.zeros(tplan_v.shape, jnp.int32)
        tplan_v[0:1, :], tplan_v[1:2, :], tplan_v[2:3, :] = order(lanes(wanted), 8)
        tplan_copy = pltpu.make_async_copy(tplan_v, tplan, idx_sem.at[2])
        tplan_copy.start()
        return tplan_copy

    known = []

    def operate(stage, fv, out, x_h, x_y, trm, fet):
        if stage == 0:
            loads[0].wait()
        halo_copies = [
            remote(fv.at[pl.ds(0, HB)], halo.at[stage, pl.ds(HB, HB)],
                   halo_send.at[stage, 0], halo_recv.at[stage, 0], left),
            remote(fv.at[pl.ds(brows - HB, HB)], halo.at[stage, pl.ds(0, HB)],
                   halo_send.at[stage, 1], halo_recv.at[stage, 1], right),
        ]

        def send_fetch(wanted):
            for d in range(N_BLK):
                for s in range(SHORT):
                    if d == 0:
                        fet[s] = fv[wanted[s]]
                    else:
                        fet_out[(d - 1) * SHORT + s] = fv[wanted[d * SHORT + s]]
            return [
                remote(fet_out.at[pl.ds((d - 1) * SHORT, SHORT)], fet.at[pl.ds((4 - d) * SHORT, SHORT)],
                       fet_send.at[stage, d - 1], fet_recv.at[stage, 3 - d], peers[d])
                for d in (1, 3, 2)
            ]

        if stage == 1:
            fet_copies = send_fetch(known[0])

        if stage == 0:
            loads[1].wait()
        terms = []
        for d in range(N_BLK):
            c = lax.rem(b + d, N_BLK)
            for s in range(SHORT):
                terms.append(three(ws[c * SHORT + s].T, jnp.concatenate(split(fv[srows[s, c]]), axis=0)))
        for s in range(SHORT):
            trm[s] = terms[s]
        for i in range(SHORT, N_BLK * SHORT):
            trm_out[i - SHORT] = terms[i]

        def send_terms(s):
            return [
                remote(trm_out.at[(d - 1) * SHORT + s], trm.at[(4 - d) * SHORT + s],
                       trm_send.at[stage, s, d - 1], trm_recv.at[stage, s, 3 - d], peers[d])
                for d in (1, 3, 2)
            ]

        trm_copies = send_terms(0)
        trm_copies += send_terms(1)
        if stage == 0:
            known.append(learn_wanted())
            fet_copies = send_fetch(known[0])
            known.append(order_wanted(known[0]))

            def spread_diag(i, c):
                for u in range(8):
                    r = i * 8 + u
                    dsp[r] = jnp.broadcast_to(diag[pl.ds(r, 1), :], (128, 128)).T * 0.5
                return c

            lax.fori_loop(0, brows // 8, spread_diag, 0)

        def split_own(i, c):
            for u in range(4):
                r = i * 4 + u
                hi, lo = split(fv[r])
                ext[HB + r, :128, :] = hi
                ext[HB + r, 128:, :] = lo
            return c

        lax.fori_loop(0, brows // 4, split_own, 0)

        acc_h[...] = jnp.zeros(acc_h.shape, F32)
        acc_l[...] = jnp.zeros(acc_l.shape, F32)
        acc_y[...] = jnp.zeros(acc_y.shape, F32)

        def halves(i):
            hi = ext[pl.ds(HB + i * per, per), :128, :].reshape(per * 128, 256)
            lo = ext[pl.ds(HB + i * per, per), 128:, :].reshape(per * 128, 256)
            return hi, lo

        def gram(i, c):
            hi, lo = halves(i)
            both = dot_t(hi, jnp.concatenate([hi, lo], axis=1))
            acc_h[...] += both[:, :256] + dot_t(lo, lo)
            acc_l[...] += both[:, 256:]
            return c

        lax.fori_loop(0, brows // per, gram, 0)
        low = acc_l[...]
        x_h[pl.ds(256 * stage, 256)] = acc_h[...] + (low + low.T)
        if stage == 0:
            reduce1.scatter()
        else:
            reduce3.scatter()
            reduce1.gather()

        if stage == 0:
            plan_copy.wait()
            known[1].wait()
            loads[2].wait()

        def backward(i, carry):
            terms = []
            for u in range(back):
                m = plan[PERM, i * back + u]
                terms.append(three(wn[m].T, ext[HB + lax.div(m, NEAR_PER)]))
            run = seg[i * back]
            for u in range(back):
                run = run * plan[KEEP, i * back + u].astype(F32) + terms[u]
                seg[i * back + u + 1] = run
            return carry

        lax.fori_loop(0, brows * NEAR_PER // back, backward, 0)
        for q in range(HB):
            rim_out[q] = seg[plan[LAST, q]]
            rim_out[HB + q] = seg[plan[LAST, HB + brows + q]]
        rim_copies = [
            remote(rim_out.at[pl.ds(0, HB)], rim_in.at[stage, pl.ds(HB, HB)],
                   rim_send.at[stage, 0], rim_recv.at[stage, 0], left),
            remote(rim_out.at[pl.ds(HB, HB)], rim_in.at[stage, pl.ds(0, HB)],
                   rim_send.at[stage, 1], rim_recv.at[stage, 1], right),
        ]

        for copy in halo_copies:
            copy.wait()
        for q in range(2 * HB):
            hi, lo = split(halo[stage, q])
            at = q if q < HB else q + brows
            ext[at, :128, :] = hi
            ext[at, 128:, :] = lo

        def half_diag(r):
            d = dsp[r]
            return jnp.concatenate([d, d], axis=1) * fv[r]

        def forward(i, c):
            sums = []
            for u in range(rows_at_once):
                lhs, rhs = [], []
                for j in range(NEAR_PER):
                    m = (i * rows_at_once + u) * NEAR_PER + j
                    hi, lo = split(wn[m])
                    e = ext[cols[m]]
                    lhs += [hi, hi, lo]
                    rhs += [e, e[:128]]
                sums.append(dot(jnp.concatenate(lhs, axis=1), jnp.concatenate(rhs, axis=0)))
            for u in range(rows_at_once):
                r = i * rows_at_once + u
                out[r] = half_diag(r) + sums[u]
            return c

        lax.fori_loop(0, brows // rows_at_once, forward, 0)
        for copy in fet_copies:
            copy.wait()
        terms = []
        for i in range(N_BLK * SHORT):
            n = plan[SPERM, i]
            slot = lax.rem(lax.div(n, SHORT) + N_BLK - b, N_BLK) * SHORT + lax.rem(n, SHORT)
            hi, lo = split(fet[slot])
            terms.append(three(ws[n], jnp.concatenate([hi, lo], axis=0)))
        run = rseg[0]
        for i in range(N_BLK * SHORT):
            run = run * plan[SKEEP, i].astype(F32) + terms[i]
            rseg[i + 1] = run

        def gram_y(i, c):
            parts = []
            for u in range(per):
                r = i * per + u
                f = out[r] + rseg[plan[SLAST, r]]
                out[r] = f
                parts.append(f)
            fh, fl = split(jnp.concatenate(parts, axis=0))
            hi, lo = halves(i)
            both = dot_t(hi, jnp.concatenate([fh, fl], axis=1))
            acc_y[...] += (both[:, :256] + both[:, 256:]) + dot_t(lo, fh)
            return c

        lax.fori_loop(0, brows // per, gram_y, 0)
        y = acc_y[...]
        x_y[pl.ds(0, 256)] = y + y.T
        if stage == 1:
            reduce2.scatter()
            reduce1.finish()
            start_inverse()
            reduce3.across()
            double_inverse(6)

        for copy in trm_copies:
            copy.wait()
        run = tseg[0]
        for i in range(N_BLK * SHORT):
            run = run * tplan[KEEP, i].astype(F32) + trm[tplan[PERM, i]]
            tseg[i + 1] = run

        def finish(i, c):
            for u in range(4):
                r = i * 4 + u
                out[r] = (out[r] + half_diag(r)) + (seg[plan[LAST, HB + r]] + tseg[tplan[LAST, r]])
            return c

        if stage == 0:
            reduce1.across()
        else:
            reduce2.across()
            reduce3.gather()
            double_inverse(4)
        lax.fori_loop(0, brows // 4, finish, 0)
        for copy in rim_copies:
            copy.wait()
        for q in range(HB):
            out[q] = out[q] + rim_in[stage, q]
            out[brows - HB + q] = out[brows - HB + q] + rim_in[stage, HB + q]

    operate(0, f0, f1, x1, x3, trm_0, fet_0)
    copy1 = pltpu.make_async_copy(f1, image, out_sem.at[0])
    copy1.start()
    operate(1, f1, f0, x3, x2, trm_1, fet_1)
    copy2 = pltpu.make_async_copy(f0, image2, out_sem.at[1])
    copy2.start()
    reduce2.gather()
    double_inverse(4)
    inverse0[...] = work[:256] * along[...] * down[...]
    reduce3.finish()
    reduce2.finish()
    copy1.wait()
    copy2.wait()


def krylov(near_cols, short_rows, short_cols, field, diag, near, short):
    brows = field.shape[0]
    smem = pl.BlockSpec(memory_space=pltpu.SMEM)
    vmem = pl.BlockSpec(memory_space=pltpu.VMEM)
    hbm = pl.BlockSpec(memory_space=pl.ANY)
    n_grp = 32
    dma = pltpu.SemaphoreType.DMA

    def block(*n):
        return pltpu.VMEM(n + (128, 256), F32)

    def words(*n):
        return pltpu.VMEM(n + (8, 128), jnp.int32)

    def reduce_scratch(n, piece):
        return [
            pltpu.VMEM((n - 1, piece, 256), F32), pltpu.VMEM((piece, 256), F32),
            pltpu.VMEM((N_BLK - 1, piece, 256), F32), pltpu.VMEM((piece, 256), F32),
        ]

    return pl.pallas_call(
        krylov_kernel,
        out_shape=(
            jax.ShapeDtypeStruct(field.shape, F32),
            jax.ShapeDtypeStruct(field.shape, F32),
            jax.ShapeDtypeStruct((256, 256), F32),
            jax.ShapeDtypeStruct((512, 256), F32),
            jax.ShapeDtypeStruct((256, 256), F32),
            jax.ShapeDtypeStruct((256, 256), F32),
        ),
        in_specs=[smem, smem, smem, vmem, hbm, vmem, hbm, hbm],
        out_specs=(hbm, hbm, vmem, vmem, vmem, vmem),
        scratch_shapes=[
            block(brows), block(brows),
            pltpu.VMEM((brows + 2 * HB, 256, 256), BF16),
            pltpu.VMEM(near.shape, F32),
            pltpu.VMEM(short.shape, F32),
            pltpu.VMEM((brows, 128, 128), F32),
            block(brows * NEAR_PER + 1), block(9), block(9),
            block(2, 2 * HB), block(2 * HB), block(2, 2 * HB),
            block(6), block(8), block(8), block(6), block(8), block(8),
            words(), words(3), pltpu.SMEM((3, 8, 128), jnp.int32), words(),
            words(), pltpu.SMEM((8, 128), jnp.int32), words(), pltpu.SMEM((8, 128), jnp.int32),
            pltpu.VMEM((256, 256), F32), pltpu.VMEM((256, 256), F32), pltpu.VMEM((256, 256), F32),
            pltpu.VMEM((256, 256), F32), *reduce_scratch(32, 8),
            pltpu.VMEM((256, 256), F32), *reduce_scratch(32, 8),
            pltpu.VMEM((512, 256), F32), *reduce_scratch(32, 16),
            pltpu.VMEM((512, 256), F32), pltpu.VMEM((1, 256), F32), pltpu.VMEM((256, 1), F32),
            dma((3,)), dma((2,)), dma((3,)), dma((3,)), dma((3,)),
            dma((2, 2)), dma((2, 2)), dma((2, 2, 3)), dma((2, 2, 3)), dma((2, 3)), dma((2, 3)),
            dma((2, 2)), dma((2, 2)),
            dma((4, n_grp - 1)), dma((2, 3)), dma((4, n_grp - 1)), dma((2, 3)), dma((4, n_grp - 1)), dma((2, 3)),
        ],
        compiler_params=pltpu.CompilerParams(
            collective_id=0, has_side_effects=True, vmem_limit_bytes=VMEM_LIMIT
        ),
        name="krylov",
    )(near_cols, short_rows.T, short_cols.T, near_cols.reshape(1, -1), field, diag, near, short)


def tail_kernel(
    grams1, grams3, grams2, inverse0, r0, q1, s2, sol, res,
    rv, qv, sv, sol_v, res_v, w_sol, w_res, work, load_sem, sol_sem, res_sem,
):
    loads = [
        pltpu.make_async_copy(src, dst, load_sem.at[i])
        for i, (src, dst) in enumerate(((r0, rv), (q1, qv), (s2, sv)))
    ]
    for copy in loads:
        copy.start()
    n = 256
    diagonal = on_diagonal()
    eye = identity()

    def size(m):
        return jnp.max(jnp.abs(m))

    def square(limit):
        def step(state):
            e = work[n:, :]
            both = mm3(work[...], e)
            work[:n, :] = work[:n, :] + both[:n]
            work[n:, :] = both[n:]
            return state[0] + 1, size(both[n:])

        return lax.while_loop(
            lambda state: (state[0] < limit) & (state[1] > 1e-5), step, (jnp.int32(0), size(work[n:, :]))
        )[1]

    def polish(m):
        def step(state):
            x = work[:n, :]
            e = eye - mm(m, x)
            work[:n, :] = x + mm(x, e)
            return state[0] + 1, size(e)

        lax.while_loop(lambda state: (state[0] < 6) & (state[1] > 1e-4), step, (jnp.int32(0), F32(1.0)))

    def spd_inverse(m, guess):
        along, down = scales(m)
        scaled = m * along * down

        def from_norm():
            bound = jnp.max(jnp.sum(jnp.abs(scaled), axis=1, keepdims=True))
            work[:n, :] = eye / bound
            work[n:, :] = eye - scaled / bound
            square(48)
            polish(scaled)

        near = guess / along / down
        z = mm(scaled, near)
        tau = n / jnp.sum(jnp.where(diagonal, z, 0.0))
        work[:n, :] = near * tau
        work[n:, :] = eye - z * tau
        left = square(6)

        @pl.when(jnp.logical_not(left <= 1e-5))
        def _():
            from_norm()

        return work[:n, :] * along * down

    def solve(matrix, inverse, rhs):
        x = mm3(inverse, rhs)
        return x + mm3(inverse, rhs - mm(matrix, x))

    rr0, g12 = grams1[...], grams2[...]
    g01, g11 = (grams3[i * n : (i + 1) * n, :] for i in range(2))
    inv0 = spd_inverse(rr0, inverse0[...])
    a1 = solve(g01, spd_inverse(g01, inv0), rr0)
    ga = mm(g01, a1)
    g11a = mm(g11, a1)
    rr1 = (rr0 - ga) + (mm(a1.T, g11a) - ga.T)
    rr1 = 0.5 * (rr1 + rr1.T)
    t = eye + solve(rr0, inv0, rr1)
    cross = mm(t.T, g11a)
    pq2 = (mm(t.T, mm(g01, t)) - cross) + (mm(a1.T, mm(g12, a1)) - cross.T)
    pq2 = 0.5 * (pq2 + pq2.T)
    a2 = solve(pq2, spd_inverse(pq2, inv0), rr1)
    c = a1 + mm(t, a2)
    d = mm(a1, a2)
    c_diag = jnp.sum(jnp.where(diagonal, c, 0.0), axis=0, keepdims=True)
    d_diag = jnp.sum(jnp.where(diagonal, d, 0.0), axis=0, keepdims=True)
    c_hi, c_lo = split(jnp.where(diagonal, 0.0, c))
    d_hi, d_lo = split(jnp.where(diagonal, 0.0, d))
    for i, part in enumerate((c_hi, c_lo, c_hi, -d_hi, -d_lo, -d_hi)):
        w_sol[i * n : (i + 1) * n, :] = part
        w_res[i * n : (i + 1) * n, :] = -part

    for copy in loads:
        copy.wait()
    tile = 512
    tiles = rv.shape[0] // tile

    def three(x, y):
        x_hi, x_lo = split(x)
        y_hi, y_lo = split(y)
        return jnp.concatenate([x_hi, x_hi, x_lo, y_hi, y_hi, y_lo], axis=1)

    for i in range(tiles):
        at = pl.ds(i * tile, tile)
        sol_v[at] = (rv[at] * c_diag - qv[at] * d_diag) + dot(three(rv[at], qv[at]), w_sol[...])
        pltpu.make_async_copy(sol_v.at[at], sol.at[at], sol_sem.at[i]).start()
        res_v[at] = (rv[at] - qv[at] * c_diag + sv[at] * d_diag) + dot(three(qv[at], sv[at]), w_res[...])
        pltpu.make_async_copy(res_v.at[at], res.at[at], res_sem.at[i]).start()
    for i in range(tiles):
        at = pl.ds(i * tile, tile)
        pltpu.make_async_copy(sol_v.at[at], sol.at[at], sol_sem.at[i]).wait()
        pltpu.make_async_copy(res_v.at[at], res.at[at], res_sem.at[i]).wait()


def tail(grams1, grams3, grams2, inverse0, r0, q1, s2):
    vmem = pl.BlockSpec(memory_space=pltpu.VMEM)
    hbm = pl.BlockSpec(memory_space=pl.ANY)
    dma = pltpu.SemaphoreType.DMA
    field = pltpu.VMEM(r0.shape, F32)
    return pl.pallas_call(
        tail_kernel,
        out_shape=(jax.ShapeDtypeStruct(r0.shape, F32),) * 2,
        in_specs=[vmem, vmem, vmem, vmem, hbm, hbm, hbm],
        out_specs=(hbm, hbm),
        scratch_shapes=[
            field, field, field, field, field,
            pltpu.VMEM((1536, 256), BF16), pltpu.VMEM((1536, 256), BF16),
            pltpu.VMEM((512, 256), F32),
            dma((3,)), dma((8,)), dma((8,)),
        ],
        compiler_params=pltpu.CompilerParams(vmem_limit_bytes=VMEM_LIMIT),
        name="tail",
    )(grams1, grams3, grams2, inverse0, r0, q1, s2)


def body(loads, pore_diag, near_blocks, near_cols, short_blocks, short_rows, short_cols):
    rows, cases = loads.shape
    brows = rows // 128
    q1, s2, grams1, grams3, grams2, inverse0 = krylov(
        near_cols, short_rows, short_cols, loads.reshape(brows, 128, cases), pore_diag.reshape(brows, 128),
        near_blocks, short_blocks.reshape(-1, 128, 128),
    )
    return tail(grams1, grams3, grams2, inverse0, loads, q1.reshape(rows, cases), s2.reshape(rows, cases))


def solution(mesh):
    in_specs = (
        P(("blk", "grp"), None),
        P(("blk", "grp")),
        P(("blk", "grp"), None, None),
        P(("blk", "grp")),
        P(("blk", "grp"), None, None, None),
        P(("blk", "grp"), None),
        P(("blk", "grp"), None),
    )
    out_specs = (P(("blk", "grp"), None), P(("blk", "grp"), None))
    return jax.shard_map(body, mesh=mesh, in_specs=in_specs, out_specs=out_specs, check_vma=False)
```
